128 devices in a mesh: wide: 32 (over x, y, core), narrow: 4 (over z).
Axes of the slice: x: 4, y: 4, z: 4, core: 2. Of those that a mesh axis runs over, the one named last changes fastest.
Arguments:
- right_side: float32 [512, 128, 512], P('wide', 'narrow'), may hold values from -18 to 18
- coef_fine: float32 [2, 512, 128, 512], P(None, 'wide', 'narrow'), may hold values from 0.05 to 1
- coef_mid: float32 [2, 256, 64, 256], P(None, 'wide', 'narrow'), may hold values from 0.05 to 1
- coef_low: float32 [2, 128, 32, 128], P(None, 'wide', 'narrow'), may hold values from 0.05 to 1
- coarse_offset: int32 [1], replicated, may hold values from 1 to 31
Outputs:
- correction: float32 [512, 128, 512], P('wide', 'narrow')
- remainder: float32 [512, 128, 512], P('wide', 'narrow')
The draws below stay inside these ranges and needn't reach their ends.
All inputs are finite; a program needn't handle non-finite values.
Results may differ from the reference program's by a relative error of at most 0.0003.
Values sent between devices are 32-bit elements; how exact they have to be, the bound alone decides.
A program may use at most 256 MiB of HBM per device.

```python
import math
import jax
import jax.numpy as jnp
from jax import lax

CX = 16
CZ = 512
NU = 2
NUC = 6
NX = 512
NY = 128
NX1 = 256
NY1 = 64
NZ1 = 256
NX2 = 128
NY2 = 32
NZ2 = 128
N_WIDE = 32


def level_of(key, dims, pieces, least, largest):
    def one(position, parts):
        heights = jax.random.uniform(jax.random.fold_in(jax.random.fold_in(key, 6), position), (parts,), jnp.float32, least / len(pieces), largest / len(pieces))
        return jnp.repeat(jnp.exp(heights), dims[position] // parts).reshape((-1,) + (1,) * (len(dims) - position - 1))

    level = one(*pieces[0])
    for cut in pieces[1:]:
        level = level * one(*cut)
    return level


def centred(own_key, dims, spread, most, pieces=(), kind=jnp.bfloat16):
    factor_of = level_of(own_key, dims, pieces, -0.22, 0.18) if pieces else 1.0
    result = jax.random.normal(own_key, dims, jnp.float32) * spread * factor_of
    return jnp.minimum(jnp.maximum(result, -most), most).astype(kind)


def setup_inputs(seed: int = 0) -> dict:
    keys = jax.random.split(jax.random.key(seed), 6)
    right_side = centred(keys[0], (NX, NY, CZ), 3.0, 18.0, ((0, 32), (1, 4)), jnp.float32)
    coef_fine = jnp.clip(jnp.exp(math.log(1.0) - 2.9957323 * jax.random.uniform(keys[1], (2, NX, NY, CZ), jnp.float32) ** level_of(keys[1], (2, NX, NY, CZ), ((1, 32), (2, 4)), -0.2, 0.2)), 0.05, 1.0)
    coef_mid = jnp.clip(jnp.exp(math.log(1.0) - 2.9957323 * jax.random.uniform(keys[2], (2, NX1, NY1, NZ1), jnp.float32) ** level_of(keys[2], (2, NX1, NY1, NZ1), ((1, 32), (2, 4)), -0.2, 0.2)), 0.05, 1.0)
    coef_low = jnp.clip(jnp.exp(math.log(1.0) - 2.9957323 * jax.random.uniform(keys[3], (2, NX2, NY2, NZ2), jnp.float32) ** level_of(keys[3], (2, NX2, NY2, NZ2), ((1, 32), (2, 4)), -0.2, 0.2)), 0.05, 1.0)
    coarse_offset = jax.random.randint(keys[4], (1,), 1, N_WIDE).astype(jnp.int32)
    return {"right_side": right_side, "coef_fine": coef_fine, "coef_mid": coef_mid, "coef_low": coef_low, "coarse_offset": coarse_offset}


def neighbours(padded):
    return (padded[:-2, 1:-1, 1:-1], padded[2:, 1:-1, 1:-1],
            padded[1:-1, :-2, 1:-1], padded[1:-1, 2:, 1:-1],
            padded[1:-1, 1:-1, :-2], padded[1:-1, 1:-1, 2:])


def face_terms(coef_pad, diag_term):
    centre = coef_pad[1:-1, 1:-1, 1:-1]
    face_list = [0.5 * (centre + beside_all) for beside_all in neighbours(coef_pad)]
    face_total = face_list[0]
    for other in face_list[1:]:
        face_total = face_total + other
    return face_list, face_total + diag_term


def pulled(face_list, iterate_pad):
    beside_all = neighbours(iterate_pad)
    summed = face_list[0] * beside_all[0]
    for place in range(1, 6):
        summed = summed + face_list[place] * beside_all[place]
    return summed


def checker(shape):
    plane_x = lax.broadcasted_iota(jnp.int32, shape, 0)
    plane_y = lax.broadcasted_iota(jnp.int32, shape, 1)
    plane_z = lax.broadcasted_iota(jnp.int32, shape, 2)
    return (plane_x + plane_y + plane_z) % 2 == 0


def relaxed(iterate, iterate_pad, source, face_list, diagonal, even_cells, colour):
    updated = (source + pulled(face_list, iterate_pad)) / diagonal
    chosen = even_cells if colour == 0 else jnp.logical_not(even_cells)
    return jnp.where(chosen, updated, iterate)


def restrict(residue):
    extent_x, extent_y, extent_z = residue.shape
    blocks = residue.reshape(extent_x // 2, 2, extent_y // 2, 2, extent_z // 2, 2)
    return 0.5 * blocks.sum(axis=(1, 3, 5))


def prolong(coarse):
    extent_x, extent_y, extent_z = coarse.shape
    spread_out = jnp.broadcast_to(coarse[:, None, :, None, :, None], (extent_x, 2, extent_y, 2, extent_z, 2))
    return spread_out.reshape(2 * extent_x, 2 * extent_y, 2 * extent_z)


def smooth(iterate, source, face_list, diagonal, repeats):
    even_cells = checker(iterate.shape)
    for repeat in range(repeats):
        for colour in (0, 1):
            iterate = relaxed(iterate, jnp.pad(iterate, 1), source, face_list, diagonal, even_cells, colour)
    return iterate


def residual(iterate, source, face_list, diagonal):
    return source - (diagonal * iterate - pulled(face_list, jnp.pad(iterate, 1)))


def reference(right_side, coef_fine, coef_mid, coef_low, coarse_offset):
    box_offset = coarse_offset[0]
    mid_coef = jnp.roll(coef_mid, -box_offset * (CX // 2), axis=1)
    low_coef = jnp.roll(coef_low, -box_offset * (CX // 4), axis=1)
    fine_faces, fine_diag = face_terms(jnp.pad(coef_fine[0], 1), coef_fine[1])
    mid_faces, mid_diag = face_terms(jnp.pad(mid_coef[0], 1), mid_coef[1])
    low_faces, low_diag = face_terms(jnp.pad(low_coef[0], 1), low_coef[1])
    fine_field = smooth(jnp.zeros_like(right_side), right_side, fine_faces, fine_diag, NU)
    mid_source = restrict(residual(fine_field, right_side, fine_faces, fine_diag))
    mid_field = smooth(jnp.zeros_like(mid_source), mid_source, mid_faces, mid_diag, NU)
    low_source = restrict(residual(mid_field, mid_source, mid_faces, mid_diag))
    low_field = smooth(jnp.zeros_like(low_source), low_source, low_faces, low_diag, NUC)
    mid_field = mid_field + prolong(low_field)
    mid_field = smooth(mid_field, mid_source, mid_faces, mid_diag, NU)
    fine_field = fine_field + prolong(mid_field)
    fine_field = smooth(fine_field, right_side, fine_faces, fine_diag, NU)
    remainder = residual(fine_field, right_side, fine_faces, fine_diag)
    return fine_field, remainder
```

```python
import jax
import jax.numpy as jnp
from jax import lax
from jax.experimental import pallas as pl
from jax.experimental.pallas import tpu as pltpu
from jax.sharding import PartitionSpec as P

MESH = pl.DeviceIdType.MESH
F32 = jnp.float32
NW, NN = 32, 4
LOW_SENDS = [(dw, dn) for dw in range(-4, 5) for dn in range(4) if (dw, dn) != (0, 0)]
CORNERS = [(dw, dn) for dw in (-1, 1) for dn in (-1, 1)]
SIDES = [(-1, 0), (1, 0), (0, -1), (0, 1)]


def iota(axis):
    return lax.broadcasted_iota(jnp.int32, (8, 128), axis)


def take(x, index):
    return jnp.take_along_axis(x, index, axis=1, mode="promise_in_bounds")


def split_index(n):
    lane = iota(1)
    width = 128 // n
    block, place = lane // width, lane % width
    return [n * place + (block - a) % n for a in range(n)], block


def split_lanes(parts, index, block):
    n = len(parts)
    gathered = [take(part, index[a]) for a, part in enumerate(parts)]
    out = []
    for t in range(n):
        tile = gathered[(n - 1 - t) % n]
        for place in range(n - 1):
            tile = jnp.where(block == place, gathered[(place - t) % n], tile)
        out.append(tile if t == 0 else pltpu.roll(tile, 128 - t * (128 // n), 1))
    return out


def join_index(n):
    lane = iota(1)
    width = 128 // n
    return [width * ((lane % n + a) % n) + lane // n for a in range(n)], lane // width


def join_lanes(tiles, index, block):
    n = len(tiles)
    turned = [tiles[t] if t == 0 else pltpu.roll(tiles[t], t * (128 // n), 1) for t in range(n)]
    out = []
    for a in range(n):
        tile = turned[(n - 1 - a) % n]
        for place in range(n - 1):
            tile = jnp.where(block == place, turned[(place - a) % n], tile)
        out.append(take(tile, index[a]))
    return out


def down(x):
    return pltpu.roll(x, 1, 0)


def up(x):
    return pltpu.roll(x, 7, 0)


def left(x):
    return pltpu.roll(x, 1, 1)


def right(x):
    return pltpu.roll(x, 127, 1)


class Level:
    def __init__(self, J, T, h, fx, fy, fz, rinv, diag, src, v):
        self.J, self.T = J, T
        self.h, self.fx, self.fy, self.fz = h, fx, fy, fz
        self.rinv, self.diag, self.src, self.v = rinv, diag, src, v

    def cells(self, parity):
        return [(j, t) for j in range(self.J) for t in range(self.T) if (j + t) % 2 == parity]

    def setup(self, b_of, c_of, first, count, plane_lo, plane_hi, row_lo, row_hi):
        J, T = self.J, self.T
        lane = iota(1)
        row = J * iota(0)
        zero = jnp.zeros((8, 128), F32)

        def fill(x, _):
            scale = jnp.where((x >= plane_lo) & (x < plane_hi), 0.5, 0.0).astype(F32)
            for j in range(J):
                inside = (row + j >= row_lo) & (row + j < row_hi)
                for t in range(T):
                    self.h[x, j, t] = jnp.where(inside, b_of(x, j, t) * scale, zero)
            return 0

        lax.fori_loop(first - 1, first + count + 1, fill, 0)

        def open_face(x):
            return jnp.where((x == plane_lo) | (x == plane_hi), 0.0, 1.0).astype(F32)

        for j in range(J):
            for t in range(T):
                self.fx[first, j, t] = (self.h[first - 1, j, t] + self.h[first, j, t]) * open_face(first)

        def build(x, _):
            h = {(j, t): self.h[x, j, t] for j in range(J) for t in range(T)}
            edge_hi = open_face(x + 1)
            for t in range(T):
                real_y = [h[j, t] + (h[j - 1, t] if j else down(h[J - 1, t])) for j in range(J)]
                real_y.append(up(real_y[0]))
                for j in range(J + 1):
                    closed = (row + j == row_lo) | (row + j == row_hi)
                    self.fy[x, j, t] = jnp.where(closed, zero, real_y[j])
                for j in range(J):
                    here = h[j, t]
                    lo_x = self.h[x - 1, j, t] + here
                    hi_x = self.h[x + 1, j, t] + here
                    self.fx[x + 1, j, t] = hi_x * edge_hi
                    if t:
                        lo_z = here + h[j, t - 1]
                        self.fz[x, j, t] = lo_z
                    else:
                        beside = jnp.where(lane == 0, zero, left(h[j, T - 1]))
                        lo_z = here + beside
                        self.fz[x, j, t] = jnp.where(lane == 0, zero, lo_z)
                    if t < T - 1:
                        hi_z = here + h[j, t + 1]
                    else:
                        beside = jnp.where(lane == 127, zero, right(h[j, 0]))
                        hi_z = here + beside
                        self.fz[x, j, T] = jnp.where(lane == 127, zero, hi_z)
                    diag = lo_x + hi_x + real_y[j] + real_y[j + 1] + lo_z + hi_z + c_of(x, j, t)
                    self.diag[x, j, t] = diag
                    self.rinv[x, j, t] = 1.0 / diag
            return 0

        lax.fori_loop(first, first + count, build, 0)

    def pulled(self, x, j, t, get):
        J, T, v = self.J, self.T, self.v
        total = self.fx[x, j, t] * v[x - 1, j, t] + self.fx[x + 1, j, t] * v[x + 1, j, t]
        total += self.fy[x, j, t] * (get(j - 1, t) if j else down(get(J - 1, t)))
        total += self.fy[x, j + 1, t] * (get(j + 1, t) if j < J - 1 else up(get(0, t)))
        total += self.fz[x, j, t] * (get(j, t - 1) if t else left(get(j, T - 1)))
        total += self.fz[x, j, t + 1] * (get(j, t + 1) if t < T - 1 else right(get(j, 0)))
        return total

    def reader(self, x):
        seen = {}

        def get(j, t):
            if (j, t) not in seen:
                seen[j, t] = self.v[x, j, t]
            return seen[j, t]

        return get

    def start(self, first, count):
        def body(i, _):
            for half in (0, 1):
                x = first + 2 * i + half
                for j, t in self.cells((first + half) % 2):
                    self.v[x, j, t] = self.src[x, j, t] * self.rinv[x, j, t]
            return 0

        lax.fori_loop(0, count // 2, body, 0)

    def half_sweep(self, colour, first, count):
        def body(i, _):
            for half in (0, 1):
                x = first + 2 * i + half
                get = self.reader(x)
                for j, t in self.cells((first + half + colour) % 2):
                    total = self.src[x, j, t] + self.pulled(x, j, t, get)
                    self.v[x, j, t] = total * self.rinv[x, j, t]
            return 0

        lax.fori_loop(0, count // 2, body, 0)

    def residual(self, x, j, t, get):
        return self.src[x, j, t] - (self.diag[x, j, t] * get(j, t) - self.pulled(x, j, t, get))

    def restrict_pair(self, x):
        sums = {}
        for half in (0, 1):
            get = self.reader(x + half)
            for j in range(self.J):
                for t in range(self.T):
                    value = self.residual(x + half, j, t, get)
                    key = (j // 2, t // 2)
                    sums[key] = sums[key] + value if key in sums else value
        return {key: 0.5 * value for key, value in sums.items()}


def kernel(rhs, cf, cm, cl, out_v, out_r,
           tb, tc, ts, tv, pk, pk5, py, py5, pc,
           fh, ffx, ffy, ffz, frinv, fdiag, fsrc, fv, stage,
           mt, st, vt, vp, mh, mfx, mfy, mfz, mrinv, mdiag, msrc, mv, mstage, lstage,
           lc, s2own, s2g, lh, lcoef, lsrc, lv, v2t,
           pkv, pkv5, pyv, pyv5, pcv,
           send, recv):
    w = lax.axis_index("wide")
    n = lax.axis_index("narrow")

    def device(dw, dn):
        return (lax.rem(w + (dw + NW), NW), lax.rem(n + (dn + NN), NN))

    barrier = pltpu.get_barrier_semaphore()
    for dw, dn in LOW_SENDS:
        pl.semaphore_signal(barrier, inc=1, device_id=device(dw, dn), device_id_type=MESH)

    count = [0]

    def remote(src, dst, dw, dn):
        k = count[0]
        count[0] += 1
        copy = pltpu.make_async_remote_copy(
            src_ref=src, dst_ref=dst, send_sem=send.at[k], recv_sem=recv.at[k],
            device_id=device(dw, dn), device_id_type=MESH)
        copy.start()
        return copy

    def landed(copies):
        for copy in copies:
            copy.wait_recv()

    everything = []

    index4, block4 = split_index(4)

    def to_split(read, target):
        def body(x, _):
            for r in range(4):
                parts = [read(x, r, a) for a in range(4)]
                for t, tile in enumerate(split_lanes(parts, index4, block4)):
                    target[6 + x, t, 8 + 8 * r:16 + 8 * r, :] = tile
            return 0

        lax.fori_loop(0, 16, body, 0)

    to_split(lambda x, r, a: cf[0, x, 8 * r:8 * r + 8, 128 * a:128 * a + 128], tb)
    to_split(lambda x, r, a: cf[1, x, 8 * r:8 * r + 8, 128 * a:128 * a + 128], tc)
    to_split(lambda x, r, a: rhs[x, 8 * r:8 * r + 8, 128 * a:128 * a + 128], ts)

    def pack(field, packed, which):
        def body(p, _):
            for t in range(4):
                for half in (0, 1):
                    x = 6 + 2 * p + half
                    packed[0, which, p, t, 4 * half:4 * half + 4, :] = field[x, t, 8:12, :]
                    packed[1, which, p, t, 4 * half:4 * half + 4, :] = field[x, t, 36:40, :]
            return 0

        lax.fori_loop(0, 8, body, 0)

    def pack_fifth(field, packed):
        for x in range(16):
            for t in range(4):
                packed[0, t, x:x + 1, :] = field[6 + x, t, 12:13, :]
                packed[1, t, x:x + 1, :] = field[6 + x, t, 35:36, :]

    def send_planes(field, layers):
        own = pl.ds(8, 32)
        return [
            remote(field.at[pl.ds(6, layers), :, own], field.at[pl.ds(22, layers), :, own], -1, 0),
            remote(field.at[pl.ds(22 - layers, layers), :, own], field.at[pl.ds(6 - layers, layers), :, own], 1, 0),
        ]

    def send_rows(packed, packed5, got, got5, got_corner):
        copies = [
            remote(packed.at[0], got.at[1], 0, -1),
            remote(packed.at[1], got.at[0], 0, 1),
            remote(packed5.at[0], got5.at[1], 0, -1),
            remote(packed5.at[1], got5.at[0], 0, 1),
        ]
        for dw, dn in CORNERS:
            side, pairs = (dn + 1) // 2, pl.ds(0 if dw < 0 else 6, 2)
            there_w, there_n = (1 - dw) // 2, (1 - dn) // 2
            copies.append(remote(packed.at[side, :, pairs], got_corner.at[2 * there_w + there_n], dw, dn))
        return copies

    def unpack(field, got, got_corner, which):
        def place(x, t, half, lower, upper):
            field[x, t, 4:8, :] = lower[4 * half:4 * half + 4]
            field[x, t, 40:44, :] = upper[4 * half:4 * half + 4]

        def body(p, _):
            for t in range(4):
                lower, upper = got[0, which, p, t], got[1, which, p, t]
                for half in (0, 1):
                    place(6 + 2 * p + half, t, half, lower, upper)
            return 0

        lax.fori_loop(0, 8, body, 0)
        for there_w in (0, 1):
            for p in range(2):
                for t in range(4):
                    lower = got_corner[2 * there_w, which, p, t]
                    upper = got_corner[2 * there_w + 1, which, p, t]
                    for half in (0, 1):
                        place((22 if there_w else 2) + 2 * p + half, t, half, lower, upper)

    def unpack_fifth(field, got5):
        for x in range(16):
            for t in range(4):
                field[6 + x, t, 3:4, :] = got5[0, t, x:x + 1, :]
                field[6 + x, t, 44:45, :] = got5[1, t, x:x + 1, :]

    pack(ts, pk, 0)
    pack(tc, pk, 1)
    pack(tb, pk, 2)
    pack_fifth(tb, pk5)

    pl.semaphore_wait(barrier, len(LOW_SENDS))

    round0 = send_planes(tb, 5) + send_planes(tc, 4) + send_planes(ts, 4)
    round0 += send_rows(pk, pk5, py, py5, pc)
    everything += round0

    index2, block2 = split_index(2)

    def split_mid(x, _):
        for which in (0, 1):
            for r in range(2):
                parts = [cm[which, x, 8 * r:8 * r + 8, 128 * a:128 * a + 128] for a in range(2)]
                for t, tile in enumerate(split_lanes(parts, index2, block2)):
                    mt[which, 8 + x, t, 8 + 8 * r:16 + 8 * r, :] = tile
        return 0

    lax.fori_loop(0, 8, split_mid, 0)

    def mid_slices(dw, dn):
        planes = pl.ds(8, 8)
        planes_there = pl.ds(8 - 8 * dw, 8)
        rows = pl.ds(8, 16) if dn == 0 else pl.ds(8 if dn < 0 else 16, 8)
        rows_there = pl.ds(8, 16) if dn == 0 else pl.ds(24 if dn < 0 else 0, 8)
        return planes, rows, planes_there, rows_there

    def send_mid(field, pair):
        copies = []
        for dw, dn in SIDES + CORNERS:
            planes, rows, planes_there, rows_there = mid_slices(dw, dn)
            if pair:
                src = field.at[:, planes, :, rows]
                dst = field.at[:, planes_there, :, rows_there]
            else:
                src = field.at[planes, :, rows]
                dst = field.at[planes_there, :, rows_there]
            copies.append(remote(src, dst, dw, dn))
        return copies

    mid_coef_copies = send_mid(mt, True)
    everything += mid_coef_copies

    def send_low(src, dst_of):
        return [remote(src, dst_of(4 - dw), dw, dn) for dw, dn in LOW_SENDS]

    low_coef_copies = send_low(cl, lambda slot: lc.at[:, pl.ds(4 * slot, 4), n])
    everything += low_coef_copies
    for which in (0, 1):
        for x in range(4):
            lc[which, 16 + x, n] = cl[which, x]

    landed(round0)
    for which, field in enumerate((ts, tc, tb)):
        unpack(field, py, pc, which)
    unpack_fifth(tb, py5)

    row_lo = lambda rows: jnp.where(n == 0, rows, 0)
    row_hi = lambda edge, last: jnp.where(n == NN - 1, edge, last)
    first_box, last_box = w == 0, w == NW - 1

    fine = Level(6, 4, fh, ffx, ffy, ffz, frinv, fdiag, fsrc, fv)
    fine.setup(
        lambda x, j, t: tb[x, t, pl.ds(j, 8, stride=6), :],
        lambda x, j, t: tc[x, t, pl.ds(j, 8, stride=6), :],
        2, 24,
        jnp.where(first_box, 6, -1), jnp.where(last_box, 22, 99),
        row_lo(8), row_hi(40, 48))

    def load_fine(x, _):
        for j in range(6):
            for t in range(4):
                fsrc[x, j, t] = ts[x, t, pl.ds(j, 8, stride=6), :]
        return 0

    lax.fori_loop(2, 26, load_fine, 0)
    fine.start(2, 24)
    fine.half_sweep(1, 3, 22)
    fine.half_sweep(0, 4, 20)
    fine.half_sweep(1, 5, 18)

    def restrict_fine(i, _):
        for (j, t), value in fine.restrict_pair(6 + 2 * i).items():
            mstage[i, t, pl.ds(4 + j, 8, stride=3), :] = value
        for t in range(2):
            st[8 + i, t, 8:24, :] = mstage[i, t, 8:24, :]
        return 0

    lax.fori_loop(0, 8, restrict_fine, 0)

    round1 = send_mid(st, False)
    everything += round1

    def store_fine(x, _):
        for j in range(6):
            for t in range(4):
                tv[x, t, pl.ds(j, 8, stride=6), :] = fv[x, j, t]
        return 0

    lax.fori_loop(6, 22, store_fine, 0)
    pack(tv, pkv, 0)
    pack_fifth(tv, pkv5)
    fine_copies = send_planes(tv, 5) + send_rows(pkv, pkv5, pyv, pyv5, pcv)
    everything += fine_copies

    landed(mid_coef_copies)
    mid = Level(4, 2, mh, mfx, mfy, mfz, mrinv, mdiag, msrc, mv)
    mid.setup(
        lambda x, j, t: mt[0, x, t, pl.ds(j, 8, stride=4), :],
        lambda x, j, t: mt[1, x, t, pl.ds(j, 8, stride=4), :],
        1, 22,
        jnp.where(first_box, 8, -1), jnp.where(last_box, 16, 99),
        row_lo(8), row_hi(24, 32))

    landed(round1)

    def load_mid(x, _):
        for j in range(4):
            for t in range(2):
                msrc[x, j, t] = st[x, t, pl.ds(j, 8, stride=4), :]
        return 0

    lax.fori_loop(2, 22, load_mid, 0)
    mid.start(4, 16)
    mid.half_sweep(1, 5, 14)
    mid.half_sweep(0, 6, 12)
    mid.half_sweep(1, 7, 10)

    def restrict_mid(i, _):
        for (j, t), value in mid.restrict_pair(8 + 2 * i).items():
            lstage[i, pl.ds(j, 8, stride=2), :] = value
        value = lstage[i, 4:12, :]
        s2own[i] = value
        s2g[16 + i, n] = value
        return 0

    lax.fori_loop(0, 4, restrict_mid, 0)

    round2 = send_low(s2own, lambda slot: s2g.at[pl.ds(4 * slot, 4), n])
    everything += round2

    def store_mid(x, _):
        for j in range(4):
            for t in range(2):
                mstage[x, t, pl.ds(j, 8, stride=4), :] = mv[8 + x, j, t]
        for t in range(2):
            vt[8 + x, t, 8:24, :] = mstage[x, t, 8:24, :]
        return 0

    lax.fori_loop(0, 8, store_mid, 0)
    mid_copies = send_mid(vt, False)
    everything += mid_copies

    landed(low_coef_copies)
    lane, sub = iota(1), iota(0)
    par = (lane + sub) % 2 == 0
    zero = jnp.zeros((8, 128), F32)
    low_lo = 16 - 4 * w
    low_hi = 16 + 4 * (NW - w)

    for r in range(4):
        lh[0, r] = zero
        lh[37, r] = zero

    def fill_low(i, _):
        scale = jnp.where((i >= low_lo) & (i < low_hi), 0.5, 0.0).astype(F32)
        for r in range(4):
            lh[1 + i, r] = lc[0, i, r] * scale
        return 0

    lax.fori_loop(0, 36, fill_low, 0)

    def open_low(i):
        return jnp.where((i == low_lo) | (i == low_hi), 0.0, 1.0).astype(F32)

    def build_low(p, _):
        i = 2 * p
        edge_lo, edge_hi = open_low(i), open_low(i + 2)
        h = [[lh[i + k, r] for r in range(4)] for k in range(4)]
        for r in range(4):
            lo_x = h[0][r] + h[1][r]
            in_x = h[1][r] + h[2][r]
            hi_x = h[2][r] + h[3][r]
            faces, diags = [], []
            for k in (1, 2):
                here = h[k][r]
                below = jnp.where(sub == 0, down(h[k][r - 1]) if r else zero, down(here))
                above = jnp.where(sub == 7, up(h[k][r + 1]) if r < 3 else zero, up(here))
                lo_y, hi_y = here + below, here + above
                lo_z = here + jnp.where(lane == 0, zero, left(here))
                hi_z = here + jnp.where(lane == 127, zero, right(here))
                out_x = lo_x if k == 1 else hi_x
                diags.append(in_x + out_x + lo_y + hi_y + lo_z + hi_z + lc[1, i + k - 1, r])
                if r == 0:
                    lo_y = jnp.where(sub == 0, zero, lo_y)
                if r == 3:
                    hi_y = jnp.where(sub == 7, zero, hi_y)
                faces.append((out_x * (edge_lo if k == 1 else edge_hi), lo_y, hi_y,
                              jnp.where(lane == 0, zero, lo_z), jnp.where(lane == 127, zero, hi_z)))
            for colour in (0, 1):
                lcoef[p, r, colour, 0] = in_x
                for k in range(5):
                    a, b = faces[colour][k], faces[1 - colour][k]
                    lcoef[p, r, colour, 1 + k] = jnp.where(par, a, b)
                lcoef[p, r, colour, 6] = 1.0 / jnp.where(par, diags[colour], diags[1 - colour])
        return 0

    lax.fori_loop(0, 18, build_low, 0)

    landed(round2)

    def load_low(p, _):
        for r in range(4):
            a, b = s2g[2 * p, r], s2g[2 * p + 1, r]
            lsrc[0, p, r] = jnp.where(par, a, b)
            lsrc[1, p, r] = jnp.where(par, b, a)
            lv[0, p, r] = lsrc[0, p, r] * lcoef[p, r, 0, 6]
        return 0

    lax.fori_loop(0, 18, load_low, 0)

    def low_half_sweep(colour, first, last):
        def body(p, _):
            other = [lv[1 - colour, p, r] for r in range(4)]
            downs = [down(value) for value in other]
            ups = [up(value) for value in other]
            for r in range(4):
                coef = lambda k: lcoef[p, r, colour, k]
                before, after = lv[1 - colour, p - 1, r], lv[1 - colour, p + 1, r]
                out = jnp.where(par, before, after) if colour == 0 else jnp.where(par, after, before)
                total = lsrc[colour, p, r] + coef(0) * other[r] + coef(1) * out
                total += coef(2) * jnp.where(sub == 0, downs[r - 1], downs[r])
                total += coef(3) * jnp.where(sub == 7, ups[(r + 1) % 4], ups[r])
                total += coef(4) * left(other[r]) + coef(5) * right(other[r])
                lv[colour, p, r] = total * coef(6)
            return 0

        lax.fori_loop(first, last + 1, body, 0)

    for k in range(2, 13):
        low_half_sweep((k + 1) % 2, k // 2, 17 - k // 2)

    for i in range(12):
        v2t[i, 0:8, :] = zero
        v2t[i, 40:48, :] = zero
    for p in range(6):
        for r in range(4):
            a, b = lv[0, 6 + p, r], lv[1, 6 + p, r]
            v2t[2 * p, 8 + 8 * r:16 + 8 * r, :] = jnp.where(par, a, b)
            v2t[2 * p + 1, 8 + 8 * r:16 + 8 * r, :] = jnp.where(par, b, a)

    landed(mid_copies)

    def correct_mid(i, _):
        for j in range(4):
            coarse = v2t[i, pl.ds(8 * n + 4 + j // 2, 8, stride=2), :]
            for half in (0, 1):
                for t in range(2):
                    x = 2 * i + half
                    mv[x, j, t] = vt[x, t, pl.ds(j, 8, stride=4), :] + coarse
        return 0

    lax.fori_loop(0, 12, correct_mid, 0)
    mid.half_sweep(0, 2, 20)
    mid.half_sweep(1, 3, 18)
    mid.half_sweep(0, 4, 16)
    mid.half_sweep(1, 5, 14)

    def spread_mid(x, _):
        for j in range(4):
            for t in range(2):
                vp[x, t, pl.ds(j, 8, stride=4), :] = mv[x, j, t]
        return 0

    lax.fori_loop(5, 19, spread_mid, 0)

    landed(fine_copies)
    unpack(tv, pyv, pcv, 0)
    unpack_fifth(tv, pyv5)

    def correct_fine(q, _):
        for j in range(3):
            for t in range(2):
                coarse = vp[q + 5, t, pl.ds(4 + j, 8, stride=3), :]
                for half in (0, 1):
                    x = 2 * q + half
                    for jj in (2 * j, 2 * j + 1):
                        for tt in (2 * t, 2 * t + 1):
                            if (half + jj + tt) % 2 == 1:
                                fv[x, jj, tt] = tv[x, tt, pl.ds(jj, 8, stride=6), :] + coarse
        return 0

    lax.fori_loop(0, 14, correct_fine, 0)
    fine.half_sweep(0, 2, 24)
    fine.half_sweep(1, 3, 22)
    fine.half_sweep(0, 4, 20)
    fine.half_sweep(1, 5, 18)

    join4, join_block4 = join_index(4)

    def finish(x, _):
        get = fine.reader(6 + x)
        for j in range(6):
            for t in range(4):
                stage[0, t, pl.ds(j, 8, stride=6), :] = get(j, t)
                stage[1, t, pl.ds(j, 8, stride=6), :] = fine.residual(6 + x, j, t, get)
        for k, out in enumerate((out_v, out_r)):
            for r in range(4):
                tiles = [stage[k, t, 8 + 8 * r:16 + 8 * r, :] for t in range(4)]
                for a, part in enumerate(join_lanes(tiles, join4, join_block4)):
                    out[x, 8 * r:8 * r + 8, 128 * a:128 * a + 128] = part
        return 0

    lax.fori_loop(0, 16, finish, 0)
    for copy in everything:
        copy.wait_send()


N_COPIES = 14 + 8 + 35 + 8 + 10 + 35 + 8


def vmem(*shape):
    return pltpu.VMEM(shape, F32)


def v_cycle(rhs, cf, cm, cl):
    vm = pl.BlockSpec(memory_space=pltpu.VMEM)
    shape = jax.ShapeDtypeStruct(rhs.shape, F32)
    fine_t = (28, 4, 48, 128)
    fine_a = (28, 6, 4, 8, 128)
    mid_t = (24, 2, 32, 128)
    mid_a = (24, 4, 2, 8, 128)
    scratch = [
        vmem(*fine_t), vmem(*fine_t), vmem(*fine_t), vmem(*fine_t),
        vmem(2, 3, 8, 4, 8, 128), vmem(2, 4, 16, 128),
        vmem(2, 3, 8, 4, 8, 128), vmem(2, 4, 16, 128), vmem(4, 3, 2, 4, 8, 128),
        vmem(*fine_a), vmem(*fine_a), vmem(28, 7, 4, 8, 128), vmem(28, 6, 5, 8, 128),
        vmem(*fine_a), vmem(*fine_a), vmem(*fine_a), vmem(*fine_a), vmem(2, 4, 48, 128),
        vmem(2, *mid_t), vmem(*mid_t), vmem(*mid_t), vmem(*mid_t),
        vmem(*mid_a), vmem(*mid_a), vmem(24, 5, 2, 8, 128), vmem(24, 4, 3, 8, 128),
        vmem(*mid_a), vmem(*mid_a), vmem(*mid_a), vmem(*mid_a),
        vmem(8, 2, 32, 128), vmem(4, 16, 128),
        vmem(2, 36, 4, 8, 128), vmem(4, 8, 128), vmem(36, 4, 8, 128), vmem(38, 4, 8, 128),
        vmem(18, 4, 2, 7, 8, 128), vmem(2, 18, 4, 8, 128), vmem(2, 18, 4, 8, 128), vmem(12, 48, 128),
        vmem(2, 1, 8, 4, 8, 128), vmem(2, 4, 16, 128),
        vmem(2, 1, 8, 4, 8, 128), vmem(2, 4, 16, 128), vmem(4, 1, 2, 4, 8, 128),
        pltpu.SemaphoreType.DMA((N_COPIES,)), pltpu.SemaphoreType.DMA((N_COPIES,)),
    ]
    return pl.pallas_call(
        kernel,
        out_shape=(shape, shape),
        in_specs=[vm] * 4,
        out_specs=(vm, vm),
        scratch_shapes=scratch,
        compiler_params=pltpu.CompilerParams(
            collective_id=0, has_side_effects=True, vmem_limit_bytes=60 * 2**20),
    )(rhs, cf, cm, cl)


def on_device(rhs, cf, cm, cl, offset):
    def moved(k):
        pairs = [((i + k) % NW, i) for i in range(NW)]
        return lambda a, b: (lax.ppermute(a, "wide", pairs), lax.ppermute(b, "wide", pairs))

    cm, cl = lax.switch(offset[0] - 1, [moved(k) for k in range(1, NW)], cm, cl)
    return v_cycle(rhs, cf, cm, cl)


def solution(mesh):
    return jax.shard_map(
        on_device,
        mesh=mesh,
        in_specs=(
            P("wide", "narrow", None),
            P(None, "wide", "narrow", None),
            P(None, "wide", "narrow", None),
            P(None, "wide", "narrow", None),
            P(),
        ),
        out_specs=(P("wide", "narrow", None), P("wide", "narrow", None)),
        check_vma=False,
    )
```

```python
import jax
import jax.numpy as jnp
from jax import lax
from jax.experimental import pallas as pl
from jax.experimental.pallas import tpu as pltpu
from jax.sharding import PartitionSpec as P

MESH = pl.DeviceIdType.MESH
F32 = jnp.float32
NW, NN = 32, 4
LOW_SENDS = [(dw, dn) for dw in (-4, 4, -2, 2, 0) for dn in (-1, 0, 1, 2)
             if (dw, dn) not in ((0, 0), (-4, 2), (4, 2))]
CORNERS = [(dw, dn) for dw in (-1, 1) for dn in (-1, 1)]
SIDES = [(-1, 0), (1, 0), (0, -1), (0, 1)]
GREETED = SIDES + CORNERS + [(-2, 0), (2, 0), (-4, 0), (4, 0)]
NEAR = [(dx, dy) for dx in range(1, 5) for dy in range(1, 5)]
CORNER_BC = [(f, dx, dy) for f in (0, 1) for dx, dy in NEAR if dx + dy <= 5 - f]
CORNER_S = [(0, dx, dy) for dx, dy in NEAR if dx + dy <= 4]
CORNER_V = [(0, dx, dy) for dx, dy in NEAR if dx + dy <= 5]


def iota(axis):
    return lax.broadcasted_iota(jnp.int32, (8, 128), axis)


def take(x, index):
    return jnp.take_along_axis(x, index, axis=1, mode="promise_in_bounds")


def split_index(n):
    lane = iota(1)
    width = 128 // n
    block, place = lane // width, lane % width
    return [n * place + (block - a) % n for a in range(n)], block


def split_lanes(parts, index, block):
    n = len(parts)
    gathered = [take(part, index[a]) for a, part in enumerate(parts)]
    out = []
    for t in range(n):
        tile = gathered[(n - 1 - t) % n]
        for place in range(n - 1):
            tile = jnp.where(block == place, gathered[(place - t) % n], tile)
        out.append(tile if t == 0 else pltpu.roll(tile, 128 - t * (128 // n), 1))
    return out


def join_index(n):
    lane = iota(1)
    width = 128 // n
    return [width * ((lane % n + a) % n) + lane // n for a in range(n)], lane // width


def join_lanes(tiles, index, block):
    n = len(tiles)
    turned = [tiles[t] if t == 0 else pltpu.roll(tiles[t], t * (128 // n), 1) for t in range(n)]
    out = []
    for a in range(n):
        tile = turned[(n - 1 - a) % n]
        for place in range(n - 1):
            tile = jnp.where(block == place, turned[(place - a) % n], tile)
        out.append(take(tile, index[a]))
    return out


def down(x):
    return pltpu.roll(x, 1, 0)


def up(x):
    return pltpu.roll(x, 7, 0)


def left(x):
    return pltpu.roll(x, 1, 1)


def right(x):
    return pltpu.roll(x, 127, 1)


class Level:
    def __init__(self, J, T, h, fx, fy, fz, rinv, diag, src, v):
        self.J, self.T = J, T
        self.h, self.fx, self.fy, self.fz = h, fx, fy, fz
        self.rinv, self.diag, self.src, self.v = rinv, diag, src, v

    def unroll(self, steps):
        return 1 if self.T == 4 else 2 if steps % 2 == 0 else 3 if steps % 3 == 0 else 1

    def cells(self, parity):
        return [(j, t) for j in range(self.J) for t in range(self.T) if (j + t) % 2 == parity]

    def setup(self, b_of, c_of, first, count, plane_lo, plane_hi, row_lo, row_hi):
        J, T = self.J, self.T
        lane = iota(1)
        row = J * iota(0)
        zero = jnp.zeros((8, 128), F32)

        def fill(x, _):
            scale = jnp.where((x >= plane_lo) & (x < plane_hi), 0.5, 0.0).astype(F32)
            for j in range(J):
                inside = (row + j >= row_lo) & (row + j < row_hi)
                for t in range(T):
                    self.h[x, j, t] = jnp.where(inside, b_of(x, j, t) * scale, zero)
            return 0

        lax.fori_loop(first - 1, first + count + 1, fill, 0)

        def open_face(x):
            return jnp.where((x == plane_lo) | (x == plane_hi), 0.0, 1.0).astype(F32)

        for j in range(J):
            for t in range(T):
                self.fx[first, j, t] = (self.h[first - 1, j, t] + self.h[first, j, t]) * open_face(first)

        def build(x, _):
            h = {(j, t): self.h[x, j, t] for j in range(J) for t in range(T)}
            edge_hi = open_face(x + 1)
            for t in range(T):
                real_y = [h[j, t] + (h[j - 1, t] if j else down(h[J - 1, t])) for j in range(J)]
                real_y.append(up(real_y[0]))
                for j in range(J + 1):
                    closed = (row + j == row_lo) | (row + j == row_hi)
                    self.fy[x, j, t] = jnp.where(closed, zero, real_y[j])
                for j in range(J):
                    here = h[j, t]
                    lo_x = self.h[x - 1, j, t] + here
                    hi_x = self.h[x + 1, j, t] + here
                    self.fx[x + 1, j, t] = hi_x * edge_hi
                    if t:
                        lo_z = here + h[j, t - 1]
                        self.fz[x, j, t] = lo_z
                    else:
                        beside = jnp.where(lane == 0, zero, left(h[j, T - 1]))
                        lo_z = here + beside
                        self.fz[x, j, t] = jnp.where(lane == 0, zero, lo_z)
                    if t < T - 1:
                        hi_z = here + h[j, t + 1]
                    else:
                        beside = jnp.where(lane == 127, zero, right(h[j, 0]))
                        hi_z = here + beside
                        self.fz[x, j, T] = jnp.where(lane == 127, zero, hi_z)
                    diag = lo_x + hi_x + real_y[j] + real_y[j + 1] + lo_z + hi_z + c_of(x, j, t)
                    self.diag[x, j, t] = diag
                    self.rinv[x, j, t] = 1.0 / diag
            return 0

        lax.fori_loop(first, first + count, build, 0, unroll=self.unroll(count))

    def pulled(self, x, j, t, colour, get):
        J, T, other = self.J, self.T, self.v[1 - colour]
        total = self.fx[x, j, t] * other[x - 1, j, t // 2] + self.fx[x + 1, j, t] * other[x + 1, j, t // 2]
        total += self.fy[x, j, t] * (get(j - 1, t) if j else down(get(J - 1, t)))
        total += self.fy[x, j + 1, t] * (get(j + 1, t) if j < J - 1 else up(get(0, t)))
        total += self.fz[x, j, t] * (get(j, t - 1) if t else left(get(j, T - 1)))
        total += self.fz[x, j, t + 1] * (get(j, t + 1) if t < T - 1 else right(get(j, 0)))
        return total

    def reader(self, x, parity):
        seen = {}

        def get(j, t):
            if (j, t) not in seen:
                seen[j, t] = self.v[(parity + j + t) % 2][x, j, t // 2]
            return seen[j, t]

        return get

    def start(self, first, count):
        def body(i, _):
            for half in (0, 1):
                x = first + 2 * i + half
                for j, t in self.cells((first + half) % 2):
                    self.v[0][x, j, t // 2] = self.src[x, j, t] * self.rinv[x, j, t]
            return 0

        lax.fori_loop(0, count // 2, body, 0, unroll=self.unroll(count // 2))

    def half_sweep(self, colour, first, count):
        def body(i, _):
            for half in (0, 1):
                x = first + 2 * i + half
                get = self.reader(x, (first + half) % 2)
                for j, t in self.cells((first + half + colour) % 2):
                    total = self.src[x, j, t] + self.pulled(x, j, t, colour, get)
                    self.v[colour][x, j, t // 2] = total * self.rinv[x, j, t]
            return 0

        lax.fori_loop(0, count // 2, body, 0, unroll=self.unroll(count // 2))

    def residual(self, x, parity, j, t, get):
        pulled = self.pulled(x, j, t, (parity + j + t) % 2, get)
        return self.src[x, j, t] - (self.diag[x, j, t] * get(j, t) - pulled)

    def restrict_pair(self, x):
        sums = {}
        for half in (0, 1):
            get = self.reader(x + half, half)
            for j in range(self.J):
                for t in range(self.T):
                    value = self.residual(x + half, half, j, t, get)
                    key = (j // 2, t // 2)
                    sums[key] = sums[key] + value if key in sums else value
        return {key: 0.5 * value for key, value in sums.items()}


def kernel(rhs_hbm, cf_hbm, cm_hbm, cl_hbm, hbm_v, hbm_r,
           rhs, cf, cm, cl, in_sem, out_sem,
           tb, tc, ts, tv, pk, pk5, pkc, pkcs, py, py5, pc, pcs,
           fh, ffx, ffy, ffz, frinv, fdiag, fsrc, fv0, fv1,
           mt, st, vt, vp, mh, mfx, mfy, mfz, mrinv, mdiag, msrc, mv0, mv1, mstage, lstage,
           lc, s2own, s2g, lh, lcoef, lsrc, lv0, lv1, v2t,
           pkv, pkv5, pkvc, pyv, pyv5, pcv,
           send, recv):
    w = lax.axis_index("wide")
    n = lax.axis_index("narrow")
    core = lax.rem(w, 2)

    def device(dw, dn):
        return (lax.rem(w + (dw + NW), NW), lax.rem(n + (dn + NN), NN))

    loads = [pltpu.make_async_copy(cf_hbm.at[0], cf.at[0], in_sem.at[0]),
             pltpu.make_async_copy(cf_hbm.at[1], cf.at[1], in_sem.at[1]),
             pltpu.make_async_copy(rhs_hbm, rhs, in_sem.at[2]),
             pltpu.make_async_copy(cm_hbm, cm, in_sem.at[3]),
             pltpu.make_async_copy(cl_hbm, cl, in_sem.at[4])]
    for load in loads:
        load.start()
    ones, zeros = jnp.ones((8, 128), F32), jnp.zeros((8, 128), F32)
    for x in (*range(8), *range(32, 40)):
        for r in range(4):
            lc[0, x, r] = ones
            lc[1, x, r] = ones
            s2g[x, r] = zeros
    barrier = pltpu.get_barrier_semaphore()
    for dw, dn in GREETED:
        pl.semaphore_signal(barrier, inc=1, device_id=device(dw, dn), device_id_type=MESH)

    count = [0]

    def remote(src, dst, dw, dn):
        k = count[0]
        count[0] += 1
        copy = pltpu.make_async_remote_copy(
            src_ref=src, dst_ref=dst, send_sem=send.at[k], recv_sem=recv.at[k],
            device_id=device(dw, dn), device_id_type=MESH)
        copy.start()
        return copy

    def landed(copies):
        for copy in copies:
            copy.wait_recv()

    everything = []

    index4, block4 = split_index(4)

    def to_split(read, target):
        def body(x, _):
            for r in range(4):
                parts = [read(x, r, a) for a in range(4)]
                for t, tile in enumerate(split_lanes(parts, index4, block4)):
                    target[6 + x, t, 8 + 8 * r:16 + 8 * r, :] = tile
            return 0

        lax.fori_loop(0, 16, body, 0)

    def pack(field, packed, which):
        def body(p, _):
            for t in range(4):
                for half in (0, 1):
                    x = 6 + 2 * p + half
                    packed[0, which, p, t, 4 * half:4 * half + 4, :] = field[x, t, 8:12, :]
                    packed[1, which, p, t, 4 * half:4 * half + 4, :] = field[x, t, 36:40, :]
            return 0

        lax.fori_loop(0, 8, body, 0)

    def pack_fifth(field, packed):
        for x in range(16):
            for t in range(4):
                packed[0, t, x:x + 1, :] = field[6 + x, t, 12:13, :]
                packed[1, t, x:x + 1, :] = field[6 + x, t, 35:36, :]

    def send_planes(field, layers):
        own = pl.ds(8, 32)
        return [
            remote(field.at[pl.ds(6, layers), :, own], field.at[pl.ds(22, layers), :, own], -1, 0),
            remote(field.at[pl.ds(22 - layers, layers), :, own], field.at[pl.ds(6 - layers, layers), :, own], 1, 0),
        ]

    def pack_corners(fields, rows, packed):
        for cw in (0, 1):
            for cn in (0, 1):
                for r, (f, dx, dy) in enumerate(rows):
                    x = 22 - dx if cw else 5 + dx
                    y = 40 - dy if cn else 7 + dy
                    for t in range(4):
                        packed[2 * cw + cn, t, r:r + 1, :] = fields[f][x, t, y:y + 1, :]

    def unpack_corners(fields, rows, got):
        for cw in (0, 1):
            for cn in (0, 1):
                for r, (f, dx, dy) in enumerate(rows):
                    x = 21 + dx if cw else 6 - dx
                    y = 39 + dy if cn else 8 - dy
                    for t in range(4):
                        fields[f][x, t, y:y + 1, :] = got[2 * cw + cn, t, r:r + 1, :]

    def send_corners(corner, got_corner):
        copies = []
        for dw, dn in CORNERS:
            here = (dw + 1) + (dn + 1) // 2
            copies.append(remote(corner.at[here], got_corner.at[3 - here], dw, dn))
        return copies

    def send_rows(packed, got):
        return [remote(packed.at[0], got.at[1], 0, -1), remote(packed.at[1], got.at[0], 0, 1)]

    def unpack(field, got, which):
        def place(x, t, half, lower, upper):
            field[x, t, 4:8, :] = lower[4 * half:4 * half + 4]
            field[x, t, 40:44, :] = upper[4 * half:4 * half + 4]

        def body(p, _):
            for t in range(4):
                lower, upper = got[0, which, p, t], got[1, which, p, t]
                for half in (0, 1):
                    place(6 + 2 * p + half, t, half, lower, upper)
            return 0

        lax.fori_loop(0, 8, body, 0)

    def unpack_fifth(field, got5):
        for x in range(16):
            for t in range(4):
                field[6 + x, t, 3:4, :] = got5[0, t, x:x + 1, :]
                field[6 + x, t, 44:45, :] = got5[1, t, x:x + 1, :]

    loads[0].wait()
    to_split(lambda x, r, a: cf[0, x, 8 * r:8 * r + 8, 128 * a:128 * a + 128], tb)
    pl.semaphore_wait(barrier, len(GREETED))
    round0_coef = send_planes(tb, 5)
    pack(tb, pk, 2)
    round0_coef += send_rows(pk.at[:, 2], py.at[:, 2])
    pack_fifth(tb, pk5)
    round0_coef += send_rows(pk5, py5)
    loads[1].wait()
    to_split(lambda x, r, a: cf[1, x, 8 * r:8 * r + 8, 128 * a:128 * a + 128], tc)
    round0_coef += send_planes(tc, 4)
    pack(tc, pk, 1)
    round0_coef += send_rows(pk.at[:, 1], py.at[:, 1])
    pack_corners((tb, tc), CORNER_BC, pkc)
    round0_coef += send_corners(pkc, pc)
    loads[2].wait()
    to_split(lambda x, r, a: rhs[x, 8 * r:8 * r + 8, 128 * a:128 * a + 128], ts)
    round0_src = send_planes(ts, 4)
    pack(ts, pk, 0)
    round0_src += send_rows(pk.at[:, 0], py.at[:, 0])
    pack_corners((ts,), CORNER_S, pkcs)
    round0_src += send_corners(pkcs, pcs)
    round0 = round0_coef + round0_src

    index2, block2 = split_index(2)

    def split_mid(x, _):
        for which in (0, 1):
            for r in range(2):
                parts = [cm[which, x, 8 * r:8 * r + 8, 128 * a:128 * a + 128] for a in range(2)]
                for t, tile in enumerate(split_lanes(parts, index2, block2)):
                    mt[which, 8 + x, t, 8 + 8 * r:16 + 8 * r, :] = tile
        return 0

    loads[3].wait()
    lax.fori_loop(0, 8, split_mid, 0)
    loads[4].wait()
    for which in (0, 1):
        for x in range(4):
            lc[which, 16 + 4 * core + x, n] = cl[which, x]

    def mid_slices(dw, dn, depth=8):
        depth = 8 if dw == 0 else depth
        planes = pl.ds(16 - depth if dw > 0 else 8, depth)
        planes_there = pl.ds(8 if dw == 0 else 16 if dw < 0 else 8 - depth, depth)
        rows = pl.ds(8, 16) if dn == 0 else pl.ds(8 if dn < 0 else 16, 8)
        rows_there = pl.ds(8, 16) if dn == 0 else pl.ds(24 if dn < 0 else 0, 8)
        return planes, rows, planes_there, rows_there

    def send_mid(field, depth):
        copies = []
        for dw, dn in SIDES + CORNERS:
            planes, rows, planes_there, rows_there = mid_slices(dw, dn, depth)
            copies.append(remote(field.at[planes, :, rows], field.at[planes_there, :, rows_there], dw, dn))
        return copies

    def send_low(src, dst_of):
        return [remote(src, dst_of(4 - dw + core), dw, dn) for dw, dn in LOW_SENDS]

    landed(round0_coef)
    unpack(tb, py, 2)
    unpack(tc, py, 1)
    unpack_fifth(tb, py5)
    unpack_corners((tb, tc), CORNER_BC, pc)

    row_lo = lambda rows: jnp.where(n == 0, rows, 0)
    row_hi = lambda edge, last: jnp.where(n == NN - 1, edge, last)
    first_box, last_box = w == 0, w == NW - 1

    fine = Level(6, 4, fh, ffx, ffy, ffz, frinv, fdiag, fsrc, (fv0, fv1))
    fine.setup(
        lambda x, j, t: tb[x, t, pl.ds(j, 8, stride=6), :],
        lambda x, j, t: tc[x, t, pl.ds(j, 8, stride=6), :],
        2, 24,
        jnp.where(first_box, 6, -1), jnp.where(last_box, 22, 99),
        row_lo(8), row_hi(40, 48))

    landed(round0_src)

    coef_rows = []
    for dn in (-1, 1):
        planes, rows, _, rows_there = mid_slices(0, dn)
        coef_rows.append(remote(mt.at[:, planes, :, rows], mt.at[:, planes, :, rows_there], 0, dn))
    for dn in (1, 3, 2):
        mine = lc.at[:, pl.ds(16 + 4 * core, 4), n]
        coef_rows.append(remote(mine, mine, 0, dn))
    everything += coef_rows

    unpack(ts, py, 0)
    unpack_corners((ts,), CORNER_S, pcs)

    def load_fine(x, _):
        for j in range(6):
            for t in range(4):
                fsrc[x, j, t] = ts[x, t, pl.ds(j, 8, stride=6), :]
        return 0

    lax.fori_loop(2, 26, load_fine, 0)
    fine.start(2, 24)
    fine.half_sweep(1, 3, 22)

    landed(coef_rows)
    mid_coef_copies = [
        remote(mt.at[:, pl.ds(8, 7)], mt.at[:, pl.ds(16, 7)], -1, 0),
        remote(mt.at[:, pl.ds(9, 7)], mt.at[:, pl.ds(1, 7)], 1, 0)]

    def send_low_coef(dw, rows):
        src = lc.at[:, pl.ds(16 + 4 * core, 4), rows]
        return remote(src, lc.at[:, pl.ds(4 * (4 - dw + core), 4), rows], dw, 0)

    low_coef_near = [send_low_coef(dw, pl.ds(0, 4)) for dw in (-2, 2)]
    everything += mid_coef_copies + low_coef_near

    fine.half_sweep(0, 4, 20)
    fine.half_sweep(1, 5, 18)

    def restrict_fine(i, _):
        for (j, t), value in fine.restrict_pair(6 + 2 * i).items():
            mstage[i, t, pl.ds(4 + j, 8, stride=3), :] = value
        for t in range(2):
            st[8 + i, t, 8:24, :] = mstage[i, t, 8:24, :]
        return 0

    lax.fori_loop(0, 8, restrict_fine, 0)

    round1 = send_mid(st, 6)
    low_coef_far = [send_low_coef(dw, pl.ds(n // 2, 3)) for dw in (-4, 4)]
    everything += round1 + low_coef_far

    landed(mid_coef_copies)
    mid = Level(4, 2, mh, mfx, mfy, mfz, mrinv, mdiag, msrc, (mv0, mv1))
    mid.setup(
        lambda x, j, t: mt[0, x, t, pl.ds(j, 8, stride=4), :],
        lambda x, j, t: mt[1, x, t, pl.ds(j, 8, stride=4), :],
        1, 22,
        jnp.where(first_box, 8, -1), jnp.where(last_box, 16, 99),
        row_lo(8), row_hi(24, 32))

    landed(round1)

    def load_mid(x, _):
        for j in range(4):
            for t in range(2):
                msrc[x, j, t] = st[x, t, pl.ds(j, 8, stride=4), :]
        return 0

    lax.fori_loop(2, 22, load_mid, 0)
    mid.start(4, 16)
    mid.half_sweep(1, 5, 14)
    mid.half_sweep(0, 6, 12)
    mid.half_sweep(1, 7, 10)

    def restrict_mid(i, _):
        for (j, t), value in mid.restrict_pair(8 + 2 * i).items():
            lstage[i, pl.ds(j, 8, stride=2), :] = value
        value = lstage[i, 4:12, :]
        s2own[i] = value
        s2g[16 + 4 * core + i, n] = value
        return 0

    lax.fori_loop(0, 4, restrict_mid, 0)

    def to_sibling(refs_of, boxes):
        copies = []
        for box in boxes:
            part = refs_of(pl.ds(8 * box + 4 * core, 4))
            k = count[0]
            count[0] += 1
            copy = pltpu.make_async_remote_copy(
                src_ref=part, dst_ref=part, send_sem=send.at[k], recv_sem=recv.at[k],
                device_id=(w + 1 - 2 * core, n), device_id_type=MESH)
            copy.start()
            copies.append(copy)
        return copies

    landed(low_coef_near + low_coef_far)
    low_coef_shared = to_sibling(lambda planes: lc.at[:, planes], range(5))
    everything += low_coef_shared

    round2 = send_low(s2own, lambda slot: s2g.at[pl.ds(4 * slot, 4), n])
    everything += round2

    def store_mid(q, _):
        for half in (0, 1):
            x = 2 * q + half
            get = mid.reader(8 + x, half)
            for j in range(4):
                for t in range(2):
                    mstage[x, t, pl.ds(j, 8, stride=4), :] = get(j, t)
            for t in range(2):
                vt[8 + x, t, 8:24, :] = mstage[x, t, 8:24, :]
        return 0

    lax.fori_loop(0, 4, store_mid, 0)
    mid_copies = send_mid(vt, 8)
    everything += mid_copies

    def store_fine(q, _):
        for half in (0, 1):
            x = 6 + 2 * q + half
            get = fine.reader(x, half)
            for j in range(6):
                for t in range(4):
                    tv[x, t, pl.ds(j, 8, stride=6), :] = get(j, t)
        return 0

    lax.fori_loop(0, 8, store_fine, 0)
    pack(tv, pkv, 0)
    pack_fifth(tv, pkv5)
    pack_corners((tv,), CORNER_V, pkvc)
    fine_copies = send_planes(tv, 5) + send_rows(pkv.at[:, 0], pyv.at[:, 0]) + send_rows(pkv5, pyv5)
    fine_copies += send_corners(pkvc, pcv)
    everything += fine_copies

    landed(low_coef_shared)
    lane, sub = iota(1), iota(0)
    par = (lane + sub) % 2 == 0
    zero = jnp.zeros((8, 128), F32)
    low_lo = 16 - 4 * (w - core)
    low_hi = low_lo + 4 * NW

    for r in range(4):
        lh[0, r] = zero
        lh[41, r] = zero

    def fill_low(i, _):
        scale = jnp.where((i >= low_lo) & (i < low_hi), 0.5, 0.0).astype(F32)
        for r in range(4):
            lh[1 + i, r] = lc[0, i, r] * scale
        return 0

    lax.fori_loop(0, 40, fill_low, 0, unroll=4)

    def open_low(i):
        return jnp.where((i == low_lo) | (i == low_hi), 0.0, 1.0).astype(F32)

    def build_low(q, _):
        p = q + 2 * core
        i = 2 * p
        edge_lo, edge_hi = open_low(i), open_low(i + 2)
        h = [[lh[i + k, r] for r in range(4)] for k in range(4)]
        for r in range(4):
            lo_x = h[0][r] + h[1][r]
            in_x = h[1][r] + h[2][r]
            hi_x = h[2][r] + h[3][r]
            faces, diags = [], []
            for k in (1, 2):
                here = h[k][r]
                below = jnp.where(sub == 0, down(h[k][r - 1]) if r else zero, down(here))
                above = jnp.where(sub == 7, up(h[k][r + 1]) if r < 3 else zero, up(here))
                lo_y, hi_y = here + below, here + above
                lo_z = here + jnp.where(lane == 0, zero, left(here))
                hi_z = here + jnp.where(lane == 127, zero, right(here))
                out_x = lo_x if k == 1 else hi_x
                diags.append(in_x + out_x + lo_y + hi_y + lo_z + hi_z + lc[1, i + k - 1, r])
                if r == 0:
                    lo_y = jnp.where(sub == 0, zero, lo_y)
                if r == 3:
                    hi_y = jnp.where(sub == 7, zero, hi_y)
                faces.append((out_x * (edge_lo if k == 1 else edge_hi), lo_y, hi_y,
                              jnp.where(lane == 0, zero, lo_z), jnp.where(lane == 127, zero, hi_z)))
            for colour in (0, 1):
                lcoef[p, r, colour, 0] = in_x
                for k in range(5):
                    a, b = faces[colour][k], faces[1 - colour][k]
                    lcoef[p, r, colour, 1 + k] = jnp.where(par, a, b)
                lcoef[p, r, colour, 6] = 1.0 / jnp.where(par, diags[colour], diags[1 - colour])
        return 0

    lax.fori_loop(0, 18, build_low, 0)

    landed([copy for copy, (dw, dn) in zip(round2, LOW_SENDS) if abs(dw) < 4])
    source_shared = to_sibling(lambda planes: s2g.at[planes], (1, 2, 3))
    landed([copy for copy, (dw, dn) in zip(round2, LOW_SENDS) if abs(dw) == 4])
    source_shared += to_sibling(lambda planes: s2g.at[planes], (0, 4))
    everything += source_shared
    landed(source_shared)

    def load_low(q, _):
        p = q + 2 * core
        for r in range(4):
            a, b = s2g[2 * p, r], s2g[2 * p + 1, r]
            lsrc[0, p, r] = jnp.where(par, a, b)
            lsrc[1, p, r] = jnp.where(par, b, a)
            lv0[p, r] = lsrc[0, p, r] * lcoef[p, r, 0, 6]
        return 0

    lax.fori_loop(0, 18, load_low, 0, unroll=2)

    def low_half_sweep(colour, first, last):
        here, there = (lv0, lv1) if colour == 0 else (lv1, lv0)

        def body(q, _):
            first_pair = first + 2 * q + 2 * core
            seen = [[there[first_pair + k, r] for r in range(4)] for k in (-1, 0, 1, 2)]
            for k in (0, 1):
                p = first_pair + k
                before, other, after = seen[k:k + 3]
                downs = [down(value) for value in other]
                ups = [up(value) for value in other]
                for r in range(4):
                    coef = lambda which: lcoef[p, r, colour, which]
                    a, b = (before, after) if colour == 0 else (after, before)
                    total = lsrc[colour, p, r] + coef(0) * other[r] + coef(1) * jnp.where(par, a[r], b[r])
                    total += coef(2) * jnp.where(sub == 0, downs[r - 1], downs[r])
                    total += coef(3) * jnp.where(sub == 7, ups[(r + 1) % 4], ups[r])
                    total += coef(4) * left(other[r]) + coef(5) * right(other[r])
                    here[p, r] = total * coef(6)
            return 0

        steps = (last + 1 - first) // 2
        lax.fori_loop(0, steps, body, 0, unroll=2 if steps % 2 == 0 else 3 if steps % 3 == 0 else 1)

    for k in range(2, 13):
        low_half_sweep((k + 1) % 2, k // 2, 17 - k // 2)

    for i in range(12):
        v2t[i, 0:8, :] = zero
        v2t[i, 40:48, :] = zero
    for p in range(6):
        for r in range(4):
            a, b = lv0[6 + 2 * core + p, r], lv1[6 + 2 * core + p, r]
            v2t[2 * p, 8 + 8 * r:16 + 8 * r, :] = jnp.where(par, a, b)
            v2t[2 * p + 1, 8 + 8 * r:16 + 8 * r, :] = jnp.where(par, b, a)

    landed(mid_copies)

    def correct_mid(i, _):
        for j in range(4):
            coarse = v2t[i, pl.ds(8 * n + 4 + j // 2, 8, stride=2), :]
            for half in (0, 1):
                for t in range(2):
                    x = 2 * i + half
                    if (half + j + t) % 2 == 1:
                        mv1[x, j, t // 2] = vt[x, t, pl.ds(j, 8, stride=4), :] + coarse
        return 0

    lax.fori_loop(0, 12, correct_mid, 0)
    mid.half_sweep(0, 2, 20)
    mid.half_sweep(1, 3, 18)
    mid.half_sweep(0, 4, 16)
    mid.half_sweep(1, 5, 14)

    def spread_mid(q, _):
        for half in (0, 1):
            x = 5 + 2 * q + half
            get = mid.reader(x, 1 - half)
            for j in range(4):
                for t in range(2):
                    vp[x, t, pl.ds(j, 8, stride=4), :] = get(j, t)
        return 0

    lax.fori_loop(0, 7, spread_mid, 0)

    landed(fine_copies)
    unpack(tv, pyv, 0)
    unpack_fifth(tv, pyv5)
    unpack_corners((tv,), CORNER_V, pcv)

    def correct_fine(q, _):
        for j in range(3):
            for t in range(2):
                coarse = vp[q + 5, t, pl.ds(4 + j, 8, stride=3), :]
                for half in (0, 1):
                    x = 2 * q + half
                    for jj in (2 * j, 2 * j + 1):
                        for tt in (2 * t, 2 * t + 1):
                            if (half + jj + tt) % 2 == 1:
                                fv1[x, jj, tt // 2] = tv[x, tt, pl.ds(jj, 8, stride=6), :] + coarse
        return 0

    lax.fori_loop(0, 14, correct_fine, 0)
    fine.half_sweep(0, 2, 24)
    fine.half_sweep(1, 3, 22)
    fine.half_sweep(0, 4, 20)
    fine.half_sweep(1, 5, 18)

    for copy in round0:
        copy.wait_send()

    def result(k, x):
        staged, hbm = ((ts, hbm_v), (tc, hbm_r))[k]
        return pltpu.make_async_copy(staged.at[6 + x, :, pl.ds(8, 32)], hbm.at[x], out_sem.at[k, x])

    def finish(q, _):
        for half in (0, 1):
            x = 2 * q + half
            get = fine.reader(6 + x, half)
            for j in range(6):
                for t in range(4):
                    ts[6 + x, t, pl.ds(j, 8, stride=6), :] = get(j, t)
                    tc[6 + x, t, pl.ds(j, 8, stride=6), :] = fine.residual(6 + x, half, j, t, get)
            result(0, x).start()
            result(1, x).start()
        return 0

    def settle(x, _):
        result(0, x).wait()
        result(1, x).wait()
        return 0

    lax.fori_loop(0, 8, finish, 0)
    lax.fori_loop(0, 16, settle, 0)
    for copy in everything:
        copy.wait_send()


def join_kernel(v_ref, r_ref, out_v, out_r):
    index, block = join_index(4)
    for tiles_ref, out in ((v_ref, out_v), (r_ref, out_r)):
        for x in range(tiles_ref.shape[0]):
            for r in range(4):
                tiles = [tiles_ref[x, t, 8 * r:8 * r + 8, :] for t in range(4)]
                for a, part in enumerate(join_lanes(tiles, index, block)):
                    out[x, 8 * r:8 * r + 8, 128 * a:128 * a + 128] = part


def join(v, r):
    shape = jax.ShapeDtypeStruct((16, 32, 512), F32)
    tiles = pl.BlockSpec((4, 4, 32, 128), lambda i: (i, 0, 0, 0))
    whole = pl.BlockSpec((4, 32, 512), lambda i: (i, 0, 0))
    return pl.pallas_call(
        join_kernel, grid=(4,), out_shape=(shape, shape),
        in_specs=[tiles] * 2, out_specs=(whole, whole),
        compiler_params=pltpu.CompilerParams(vmem_limit_bytes=16 * 2**20),
    )(v, r)


N_COPIES = 14 + 8 + 5 + 6 + 8 + 10 + 5 + 17 + 8 + 5


def vmem(*shape):
    return pltpu.VMEM(shape, F32)


def v_cycle(rhs, cf, cm, cl):
    hbm = pl.BlockSpec(memory_space=pl.ANY)
    shape = jax.ShapeDtypeStruct((16, 4, 32, 128), F32)
    fine_t = (28, 4, 48, 128)
    fine_a = (28, 6, 4, 8, 128)
    mid_t = (24, 2, 32, 128)
    mid_a = (24, 4, 2, 8, 128)
    scratch = [
        vmem(*rhs.shape), vmem(*cf.shape), vmem(*cm.shape), vmem(*cl.shape),
        pltpu.SemaphoreType.DMA((5,)), pltpu.SemaphoreType.DMA((2, 16)),
        vmem(*fine_t), vmem(*fine_t), vmem(*fine_t), vmem(*fine_t),
        vmem(2, 3, 8, 4, 8, 128), vmem(2, 4, 16, 128), vmem(4, 4, 16, 128), vmem(4, 4, 8, 128),
        vmem(2, 3, 8, 4, 8, 128), vmem(2, 4, 16, 128), vmem(4, 4, 16, 128), vmem(4, 4, 8, 128),
        vmem(*fine_a), vmem(*fine_a), vmem(28, 7, 4, 8, 128), vmem(28, 6, 5, 8, 128),
        vmem(*fine_a), vmem(*fine_a), vmem(*fine_a), vmem(28, 6, 2, 8, 128), vmem(28, 6, 2, 8, 128),
        vmem(2, *mid_t), vmem(*mid_t), vmem(*mid_t), vmem(*mid_t),
        vmem(*mid_a), vmem(*mid_a), vmem(24, 5, 2, 8, 128), vmem(24, 4, 3, 8, 128),
        vmem(*mid_a), vmem(*mid_a), vmem(*mid_a), vmem(24, 4, 1, 8, 128), vmem(24, 4, 1, 8, 128),
        vmem(8, 2, 32, 128), vmem(4, 16, 128),
        vmem(2, 40, 4, 8, 128), vmem(4, 8, 128), vmem(40, 4, 8, 128), vmem(42, 4, 8, 128),
        vmem(20, 4, 2, 7, 8, 128), vmem(2, 20, 4, 8, 128), vmem(20, 4, 8, 128), vmem(20, 4, 8, 128), vmem(12, 48, 128),
        vmem(2, 1, 8, 4, 8, 128), vmem(2, 4, 16, 128), vmem(4, 4, 16, 128),
        vmem(2, 1, 8, 4, 8, 128), vmem(2, 4, 16, 128), vmem(4, 4, 16, 128),
        pltpu.SemaphoreType.DMA((N_COPIES,)), pltpu.SemaphoreType.DMA((N_COPIES,)),
    ]
    return pl.pallas_call(
        kernel,
        out_shape=(shape, shape),
        in_specs=[hbm] * 4,
        out_specs=(hbm, hbm),
        scratch_shapes=scratch,
        compiler_params=pltpu.CompilerParams(
            collective_id=0, has_side_effects=True, vmem_limit_bytes=60 * 2**20),
    )(rhs, cf, cm, cl)


def on_device(rhs, cf, cm, cl, offset):
    def moved(k):
        pairs = [((i + k) % NW, i) for i in range(NW)]
        return lambda a, b: (lax.ppermute(a, "wide", pairs), lax.ppermute(b, "wide", pairs))

    cm, cl = lax.switch(offset[0] - 1, [moved(k) for k in range(1, NW)], cm, cl)
    return join(*v_cycle(rhs, cf, cm, cl))


def solution(mesh):
    return jax.shard_map(
        on_device,
        mesh=mesh,
        in_specs=(
            P("wide", "narrow", None),
            P(None, "wide", "narrow", None),
            P(None, "wide", "narrow", None),
            P(None, "wide", "narrow", None),
            P(),
        ),
        out_specs=(P("wide", "narrow", None), P("wide", "narrow", None)),
        check_vma=False,
    )
```

```python
import functools

import jax
import jax.numpy as jnp
from jax import lax
from jax.experimental import pallas as pl
from jax.experimental.pallas import tpu as pltpu
from jax.sharding import PartitionSpec as P

MESH = pl.DeviceIdType.MESH
F32 = jnp.float32
NW, NN = 32, 4
LOW_SENDS = [(dw, dn) for dw in (-4, 4, -2, 2, 0) for dn in (-1, 0, 1, 2)
             if (dw, dn) not in ((0, 0), (-4, 2), (4, 2))]
CORNERS = [(dw, dn) for dw in (-1, 1) for dn in (-1, 1)]
SIDES = [(-1, 0), (1, 0), (0, -1), (0, 1)]
GREETED = SIDES + CORNERS + [(-2, 0), (2, 0), (-4, 0), (4, 0)]
NEAR = [(dx, dy) for dx in range(1, 5) for dy in range(1, 5)]
CORNER_BC = [(f, dx, dy) for f in (0, 1) for dx, dy in NEAR if dx + dy <= 5 - f]
CORNER_S = [(0, dx, dy) for dx, dy in NEAR if dx + dy <= 4]
CORNER_V = [(0, dx, dy) for dx, dy in NEAR if dx + dy <= 5]


def iota(axis):
    return lax.broadcasted_iota(jnp.int32, (8, 128), axis)


def take(x, index):
    return jnp.take_along_axis(x, index, axis=1, mode="promise_in_bounds")


def swap(first, second, bit):
    low = iota(1) & bit == 0
    return (jnp.where(low, first, pltpu.roll(second, bit, 1)),
            jnp.where(low, pltpu.roll(first, 128 - bit, 1), second))


def split_lanes(parts):
    a, b = swap(parts[0], parts[1], 1)
    c, d = swap(parts[2], parts[3], 1)
    (a, c), (b, d) = swap(a, c, 2), swap(b, d, 2)
    return [a, b, c, d]


def join_lanes(tiles):
    a, b, c, d = tiles
    (a, c), (b, d) = swap(a, c, 2), swap(b, d, 2)
    a, b = swap(a, b, 1)
    c, d = swap(c, d, 1)
    return [a, b, c, d]


def place_index():
    lane = iota(1)
    return 32 * (lane % 4) + lane // 4


def down(x):
    return pltpu.roll(x, 1, 0)


def up(x):
    return pltpu.roll(x, 7, 0)


def left(x):
    return jnp.where(iota(1) < 4, pltpu.roll(x, 5, 1), pltpu.roll(x, 4, 1))


def right(x):
    return jnp.where(iota(1) >= 124, pltpu.roll(x, 123, 1), pltpu.roll(x, 124, 1))


class Level:
    def __init__(self, J, T, h, fx, fy, fz, rinv, diag, src, v):
        self.J, self.T = J, T
        self.h, self.fx, self.fy, self.fz = h, fx, fy, fz
        self.rinv, self.diag, self.src, self.v = rinv, diag, src, v

    def unroll(self, steps):
        return 1 if self.T == 4 else 2 if steps % 2 == 0 else 3 if steps % 3 == 0 else 1

    def cells(self, parity):
        return [(j, t) for j in range(self.J) for t in range(self.T) if (j + t) % 2 == parity]

    def setup(self, b_of, c_of, first, count, plane_lo, plane_hi, row_lo, row_hi):
        J, T = self.J, self.T
        lane = iota(1)
        row = J * iota(0)
        zero = jnp.zeros((8, 128), F32)

        def fill(x, _):
            scale = jnp.where((x >= plane_lo) & (x < plane_hi), 0.5, 0.0).astype(F32)
            for j in range(J):
                inside = (row + j >= row_lo) & (row + j < row_hi)
                for t in range(T):
                    self.h[x, j, t] = jnp.where(inside, b_of(x, j, t) * scale, zero)
            return 0

        lax.fori_loop(first - 1, first + count + 1, fill, 0)

        def open_face(x):
            return jnp.where((x == plane_lo) | (x == plane_hi), 0.0, 1.0).astype(F32)

        for j in range(J):
            for t in range(T):
                self.fx[first, j, t] = (self.h[first - 1, j, t] + self.h[first, j, t]) * open_face(first)

        def build(x, _):
            h = {(j, t): self.h[x, j, t] for j in range(J) for t in range(T)}
            edge_hi = open_face(x + 1)
            for t in range(T):
                real_y = [h[j, t] + (h[j - 1, t] if j else down(h[J - 1, t])) for j in range(J)]
                real_y.append(up(real_y[0]))
                for j in range(J + 1):
                    closed = (row + j == row_lo) | (row + j == row_hi)
                    self.fy[x, j, t] = jnp.where(closed, zero, real_y[j])
                for j in range(J):
                    here = h[j, t]
                    lo_x = self.h[x - 1, j, t] + here
                    hi_x = self.h[x + 1, j, t] + here
                    self.fx[x + 1, j, t] = hi_x * edge_hi
                    if t:
                        lo_z = here + h[j, t - 1]
                        self.fz[x, j, t] = lo_z
                    else:
                        beside = jnp.where(lane == 0, zero, left(h[j, T - 1]))
                        lo_z = here + beside
                        self.fz[x, j, t] = jnp.where(lane == 0, zero, lo_z)
                    if t < T - 1:
                        hi_z = here + h[j, t + 1]
                    else:
                        beside = jnp.where(lane == 127, zero, right(h[j, 0]))
                        hi_z = here + beside
                        self.fz[x, j, T] = jnp.where(lane == 127, zero, hi_z)
                    diag = lo_x + hi_x + real_y[j] + real_y[j + 1] + lo_z + hi_z + c_of(x, j, t)
                    self.diag[x, j, t] = diag
                    self.rinv[x, j, t] = 1.0 / diag
            return 0

        lax.fori_loop(first, first + count, build, 0, unroll=self.unroll(count))

    def pulled(self, x, j, t, colour, get):
        J, T, other = self.J, self.T, self.v[1 - colour]
        total = self.fx[x, j, t] * other[x - 1, j, t // 2] + self.fx[x + 1, j, t] * other[x + 1, j, t // 2]
        total += self.fy[x, j, t] * (get(j - 1, t) if j else down(get(J - 1, t)))
        total += self.fy[x, j + 1, t] * (get(j + 1, t) if j < J - 1 else up(get(0, t)))
        total += self.fz[x, j, t] * (get(j, t - 1) if t else left(get(j, T - 1)))
        total += self.fz[x, j, t + 1] * (get(j, t + 1) if t < T - 1 else right(get(j, 0)))
        return total

    def reader(self, x, parity):
        seen = {}

        def get(j, t):
            if (j, t) not in seen:
                seen[j, t] = self.v[(parity + j + t) % 2][x, j, t // 2]
            return seen[j, t]

        return get

    def start(self, first, count):
        def body(i, _):
            for half in (0, 1):
                x = first + 2 * i + half
                for j, t in self.cells((first + half) % 2):
                    self.v[0][x, j, t // 2] = self.src[x, j, t] * self.rinv[x, j, t]
            return 0

        lax.fori_loop(0, count // 2, body, 0, unroll=self.unroll(count // 2))

    def half_sweep(self, colour, first, count):
        def body(i, _):
            for half in (0, 1):
                x = first + 2 * i + half
                get = self.reader(x, (first + half) % 2)
                for j, t in self.cells((first + half + colour) % 2):
                    total = self.src[x, j, t] + self.pulled(x, j, t, colour, get)
                    self.v[colour][x, j, t // 2] = total * self.rinv[x, j, t]
            return 0

        lax.fori_loop(0, count // 2, body, 0, unroll=self.unroll(count // 2))

    def residual(self, x, parity, j, t, get):
        pulled = self.pulled(x, j, t, (parity + j + t) % 2, get)
        return self.src[x, j, t] - (self.diag[x, j, t] * get(j, t) - pulled)

    def restrict_pair(self, x):
        sums = {}
        for half in (0, 1):
            get = self.reader(x + half, half)
            for j in range(self.J):
                for t in range(self.T):
                    value = self.residual(x + half, half, j, t, get)
                    key = (j // 2, t // 2)
                    sums[key] = sums[key] + value if key in sums else value
        return {key: 0.5 * value for key, value in sums.items()}


def kernel(rhs_hbm, cf_hbm, cm_hbm, cl_hbm, hbm_v, hbm_r,
           rhs, cf, cm, cl, in_sem, out_sem,
           tb, tc, ts, tv, pk, pk5, pkc, pkcs, py, py5, pc, pcs,
           fh, ffx, ffy, ffz, frinv, fdiag, fsrc, fv0, fv1,
           mt, st, vt, vp, mh, mfx, mfy, mfz, mrinv, mdiag, msrc, mv0, mv1, mstage, lstage,
           lc, s2own, s2g, lh, lcoef, lsrc, lv0, lv1, v2t,
           pkv, pkv5, pkvc, pyv, pyv5, pcv,
           send, recv):
    w = lax.axis_index("wide")
    n = lax.axis_index("narrow")
    core = lax.rem(w, 2)

    def device(dw, dn):
        return (lax.rem(w + (dw + NW), NW), lax.rem(n + (dn + NN), NN))

    loads = [pltpu.make_async_copy(cf_hbm.at[0], cf.at[0], in_sem.at[0]),
             pltpu.make_async_copy(cf_hbm.at[1], cf.at[1], in_sem.at[1]),
             pltpu.make_async_copy(rhs_hbm, rhs, in_sem.at[2]),
             pltpu.make_async_copy(cm_hbm, cm, in_sem.at[3]),
             pltpu.make_async_copy(cl_hbm, cl, in_sem.at[4])]
    for load in loads:
        load.start()
    ones, zeros = jnp.ones((8, 128), F32), jnp.zeros((8, 128), F32)
    for x in (*range(8), *range(32, 40)):
        for r in range(4):
            lc[0, x, r] = ones
            lc[1, x, r] = ones
            s2g[x, r] = zeros
    barrier = pltpu.get_barrier_semaphore()
    for dw, dn in GREETED:
        pl.semaphore_signal(barrier, inc=1, device_id=device(dw, dn), device_id_type=MESH)

    count = [0]

    def remote(src, dst, dw, dn):
        k = count[0]
        count[0] += 1
        copy = pltpu.make_async_remote_copy(
            src_ref=src, dst_ref=dst, send_sem=send.at[k], recv_sem=recv.at[k],
            device_id=device(dw, dn), device_id_type=MESH)
        copy.start()
        return copy

    def landed(copies):
        for copy in copies:
            copy.wait_recv()

    everything = []

    def to_split(read, target):
        def body(x, _):
            for r in range(4):
                parts = [read(x, r, a) for a in range(4)]
                for t, tile in enumerate(split_lanes(parts)):
                    target[6 + x, t, 8 + 8 * r:16 + 8 * r, :] = tile
            return 0

        lax.fori_loop(0, 16, body, 0)

    def pack(field, packed, which):
        def body(p, _):
            for t in range(4):
                for half in (0, 1):
                    x = 6 + 2 * p + half
                    packed[0, which, p, t, 4 * half:4 * half + 4, :] = field[x, t, 8:12, :]
                    packed[1, which, p, t, 4 * half:4 * half + 4, :] = field[x, t, 36:40, :]
            return 0

        lax.fori_loop(0, 8, body, 0)

    def pack_fifth(field, packed):
        for x in range(16):
            for t in range(4):
                packed[0, t, x:x + 1, :] = field[6 + x, t, 12:13, :]
                packed[1, t, x:x + 1, :] = field[6 + x, t, 35:36, :]

    def send_planes(field, layers):
        own = pl.ds(8, 32)
        return [
            remote(field.at[pl.ds(6, layers), :, own], field.at[pl.ds(22, layers), :, own], -1, 0),
            remote(field.at[pl.ds(22 - layers, layers), :, own], field.at[pl.ds(6 - layers, layers), :, own], 1, 0),
        ]

    def pack_corners(fields, rows, packed):
        for cw in (0, 1):
            for cn in (0, 1):
                for r, (f, dx, dy) in enumerate(rows):
                    x = 22 - dx if cw else 5 + dx
                    y = 40 - dy if cn else 7 + dy
                    for t in range(4):
                        packed[2 * cw + cn, t, r:r + 1, :] = fields[f][x, t, y:y + 1, :]

    def unpack_corners(fields, rows, got):
        for cw in (0, 1):
            for cn in (0, 1):
                for r, (f, dx, dy) in enumerate(rows):
                    x = 21 + dx if cw else 6 - dx
                    y = 39 + dy if cn else 8 - dy
                    for t in range(4):
                        fields[f][x, t, y:y + 1, :] = got[2 * cw + cn, t, r:r + 1, :]

    def send_corners(corner, got_corner):
        copies = []
        for dw, dn in CORNERS:
            here = (dw + 1) + (dn + 1) // 2
            copies.append(remote(corner.at[here], got_corner.at[3 - here], dw, dn))
        return copies

    def send_rows(packed, got):
        return [remote(packed.at[0], got.at[1], 0, -1), remote(packed.at[1], got.at[0], 0, 1)]

    def unpack(field, got, which):
        def place(x, t, half, lower, upper):
            field[x, t, 4:8, :] = lower[4 * half:4 * half + 4]
            field[x, t, 40:44, :] = upper[4 * half:4 * half + 4]

        def body(p, _):
            for t in range(4):
                lower, upper = got[0, which, p, t], got[1, which, p, t]
                for half in (0, 1):
                    place(6 + 2 * p + half, t, half, lower, upper)
            return 0

        lax.fori_loop(0, 8, body, 0)

    def unpack_fifth(field, got5):
        for x in range(16):
            for t in range(4):
                field[6 + x, t, 3:4, :] = got5[0, t, x:x + 1, :]
                field[6 + x, t, 44:45, :] = got5[1, t, x:x + 1, :]

    loads[0].wait()
    to_split(lambda x, r, a: cf[0, x, 8 * r:8 * r + 8, 128 * a:128 * a + 128], tb)
    pl.semaphore_wait(barrier, len(GREETED))
    round0_coef = send_planes(tb, 5)
    pack(tb, pk, 2)
    round0_coef += send_rows(pk.at[:, 2], py.at[:, 2])
    pack_fifth(tb, pk5)
    round0_coef += send_rows(pk5, py5)
    loads[1].wait()
    to_split(lambda x, r, a: cf[1, x, 8 * r:8 * r + 8, 128 * a:128 * a + 128], tc)
    round0_coef += send_planes(tc, 4)
    pack(tc, pk, 1)
    round0_coef += send_rows(pk.at[:, 1], py.at[:, 1])
    pack_corners((tb, tc), CORNER_BC, pkc)
    round0_coef += send_corners(pkc, pc)
    loads[2].wait()
    to_split(lambda x, r, a: rhs[x, 8 * r:8 * r + 8, 128 * a:128 * a + 128], ts)
    round0_src = send_planes(ts, 4)
    pack(ts, pk, 0)
    round0_src += send_rows(pk.at[:, 0], py.at[:, 0])
    pack_corners((ts,), CORNER_S, pkcs)
    round0_src += send_corners(pkcs, pcs)
    round0 = round0_coef + round0_src

    place = place_index()

    def split_mid(x, _):
        for which in (0, 1):
            for r in range(2):
                low, high = [cm[which, x, 8 * r:8 * r + 8, 128 * a:128 * a + 128] for a in range(2)]
                for t in range(2):
                    index = (2 * place + t) % 128
                    tile = jnp.where(place < 64, take(low, index), take(high, index))
                    mt[which, 8 + x, t, 8 + 8 * r:16 + 8 * r, :] = tile
        return 0

    loads[3].wait()
    lax.fori_loop(0, 8, split_mid, 0)
    loads[4].wait()
    for which in (0, 1):
        for x in range(4):
            lc[which, 16 + 4 * core + x, n] = take(cl[which, x], place)

    def mid_slices(dw, dn, depth=8):
        depth = 8 if dw == 0 else depth
        planes = pl.ds(16 - depth if dw > 0 else 8, depth)
        planes_there = pl.ds(8 if dw == 0 else 16 if dw < 0 else 8 - depth, depth)
        rows = pl.ds(8, 16) if dn == 0 else pl.ds(8 if dn < 0 else 16, 8)
        rows_there = pl.ds(8, 16) if dn == 0 else pl.ds(24 if dn < 0 else 0, 8)
        return planes, rows, planes_there, rows_there

    def send_mid(field, depth):
        copies = []
        for dw, dn in SIDES + CORNERS:
            planes, rows, planes_there, rows_there = mid_slices(dw, dn, depth)
            copies.append(remote(field.at[planes, :, rows], field.at[planes_there, :, rows_there], dw, dn))
        return copies

    def send_low(src, dst_of):
        return [remote(src, dst_of(4 - dw + core), dw, dn) for dw, dn in LOW_SENDS]

    landed(round0_coef)
    mid_coef_copies = []
    for dw, dn in SIDES + CORNERS:
        planes, rows, planes_there, rows_there = mid_slices(dw, dn, 7)
        mid_coef_copies.append(remote(mt.at[:, planes, :, rows], mt.at[:, planes_there, :, rows_there], dw, dn))
    everything += mid_coef_copies
    unpack(tb, py, 2)
    unpack(tc, py, 1)
    unpack_fifth(tb, py5)
    unpack_corners((tb, tc), CORNER_BC, pc)

    row_lo = lambda rows: jnp.where(n == 0, rows, 0)
    row_hi = lambda edge, last: jnp.where(n == NN - 1, edge, last)
    first_box, last_box = w == 0, w == NW - 1

    fine = Level(6, 4, fh, ffx, ffy, ffz, frinv, fdiag, fsrc, (fv0, fv1))
    fine.setup(
        lambda x, j, t: tb[x, t, pl.ds(j, 8, stride=6), :],
        lambda x, j, t: tc[x, t, pl.ds(j, 8, stride=6), :],
        2, 24,
        jnp.where(first_box, 6, -1), jnp.where(last_box, 22, 99),
        row_lo(8), row_hi(40, 48))

    landed(round0_src)

    coef_rows = []
    for dn in (1, 3, 2):
        mine = lc.at[:, pl.ds(16 + 4 * core, 4), n]
        coef_rows.append(remote(mine, mine, 0, dn))
    everything += coef_rows

    unpack(ts, py, 0)
    unpack_corners((ts,), CORNER_S, pcs)

    def load_fine(x, _):
        for j in range(6):
            for t in range(4):
                fsrc[x, j, t] = ts[x, t, pl.ds(j, 8, stride=6), :]
        return 0

    lax.fori_loop(2, 26, load_fine, 0)
    fine.start(2, 24)
    fine.half_sweep(1, 3, 22)

    landed(coef_rows)
    def send_low_coef(dw, rows):
        src = lc.at[:, pl.ds(16 + 4 * core, 4), rows]
        return remote(src, lc.at[:, pl.ds(4 * (4 - dw + core), 4), rows], dw, 0)

    low_coef_near = [send_low_coef(dw, pl.ds(0, 4)) for dw in (-2, 2)]
    everything += low_coef_near

    fine.half_sweep(0, 4, 20)
    fine.half_sweep(1, 5, 18)

    def restrict_fine(i, _):
        for (j, t), value in fine.restrict_pair(6 + 2 * i).items():
            mstage[i, t, pl.ds(4 + j, 8, stride=3), :] = value
        for t in range(2):
            st[8 + i, t, 8:24, :] = mstage[i, t, 8:24, :]
        return 0

    lax.fori_loop(0, 8, restrict_fine, 0)

    round1 = send_mid(st, 6)
    low_coef_far = [send_low_coef(dw, pl.ds(n // 2, 3)) for dw in (-4, 4)]
    everything += round1 + low_coef_far

    landed(mid_coef_copies)
    mid = Level(4, 2, mh, mfx, mfy, mfz, mrinv, mdiag, msrc, (mv0, mv1))
    mid.setup(
        lambda x, j, t: mt[0, x, t, pl.ds(j, 8, stride=4), :],
        lambda x, j, t: mt[1, x, t, pl.ds(j, 8, stride=4), :],
        1, 22,
        jnp.where(first_box, 8, -1), jnp.where(last_box, 16, 99),
        row_lo(8), row_hi(24, 32))

    landed(round1)

    def load_mid(x, _):
        for j in range(4):
            for t in range(2):
                msrc[x, j, t] = st[x, t, pl.ds(j, 8, stride=4), :]
        return 0

    lax.fori_loop(2, 22, load_mid, 0)
    mid.start(4, 16)
    mid.half_sweep(1, 5, 14)
    mid.half_sweep(0, 6, 12)
    mid.half_sweep(1, 7, 10)

    def restrict_mid(i, _):
        for (j, t), value in mid.restrict_pair(8 + 2 * i).items():
            lstage[i, pl.ds(j, 8, stride=2), :] = value
        value = lstage[i, 4:12, :]
        s2own[i] = value
        s2g[16 + 4 * core + i, n] = value
        return 0

    lax.fori_loop(0, 4, restrict_mid, 0)

    def to_sibling(refs_of, boxes):
        copies = []
        for box in boxes:
            part = refs_of(pl.ds(8 * box + 4 * core, 4))
            k = count[0]
            count[0] += 1
            copy = pltpu.make_async_remote_copy(
                src_ref=part, dst_ref=part, send_sem=send.at[k], recv_sem=recv.at[k],
                device_id=(w + 1 - 2 * core, n), device_id_type=MESH)
            copy.start()
            copies.append(copy)
        return copies

    landed(low_coef_near + low_coef_far)
    low_coef_shared = to_sibling(lambda planes: lc.at[:, planes], range(5))
    everything += low_coef_shared

    round2 = send_low(s2own, lambda slot: s2g.at[pl.ds(4 * slot, 4), n])
    everything += round2

    def store_mid(q, _):
        for half in (0, 1):
            x = 2 * q + half
            get = mid.reader(8 + x, half)
            for j in range(4):
                for t in range(2):
                    mstage[x, t, pl.ds(j, 8, stride=4), :] = get(j, t)
            for t in range(2):
                vt[8 + x, t, 8:24, :] = mstage[x, t, 8:24, :]
        return 0

    lax.fori_loop(0, 4, store_mid, 0)
    mid_copies = send_mid(vt, 8)
    everything += mid_copies

    def store_fine(q, _):
        for half in (0, 1):
            x = 6 + 2 * q + half
            get = fine.reader(x, half)
            for j in range(6):
                for t in range(4):
                    tv[x, t, pl.ds(j, 8, stride=6), :] = get(j, t)
        return 0

    lax.fori_loop(0, 8, store_fine, 0)
    pack(tv, pkv, 0)
    pack_fifth(tv, pkv5)
    pack_corners((tv,), CORNER_V, pkvc)
    fine_copies = send_planes(tv, 5) + send_rows(pkv.at[:, 0], pyv.at[:, 0]) + send_rows(pkv5, pyv5)
    fine_copies += send_corners(pkvc, pcv)
    everything += fine_copies

    landed(low_coef_shared)
    lane, sub = iota(1), iota(0)
    par = (lane // 4 + sub) % 2 == 0
    zero = jnp.zeros((8, 128), F32)
    low_lo = 16 - 4 * (w - core)
    low_hi = low_lo + 4 * NW

    for r in range(4):
        lh[0, r] = zero
        lh[41, r] = zero

    def fill_low(i, _):
        scale = jnp.where((i >= low_lo) & (i < low_hi), 0.5, 0.0).astype(F32)
        for r in range(4):
            lh[1 + i, r] = lc[0, i, r] * scale
        return 0

    lax.fori_loop(0, 40, fill_low, 0, unroll=4)

    def open_low(i):
        return jnp.where((i == low_lo) | (i == low_hi), 0.0, 1.0).astype(F32)

    def build_low(q, _):
        p = q + 2 * core
        i = 2 * p
        edge_lo, edge_hi = open_low(i), open_low(i + 2)
        h = [[lh[i + k, r] for r in range(4)] for k in range(4)]
        for r in range(4):
            lo_x = h[0][r] + h[1][r]
            in_x = h[1][r] + h[2][r]
            hi_x = h[2][r] + h[3][r]
            faces, diags = [], []
            for k in (1, 2):
                here = h[k][r]
                below = jnp.where(sub == 0, down(h[k][r - 1]) if r else zero, down(here))
                above = jnp.where(sub == 7, up(h[k][r + 1]) if r < 3 else zero, up(here))
                lo_y, hi_y = here + below, here + above
                lo_z = here + jnp.where(lane == 0, zero, left(here))
                hi_z = here + jnp.where(lane == 127, zero, right(here))
                out_x = lo_x if k == 1 else hi_x
                diags.append(in_x + out_x + lo_y + hi_y + lo_z + hi_z + lc[1, i + k - 1, r])
                if r == 0:
                    lo_y = jnp.where(sub == 0, zero, lo_y)
                if r == 3:
                    hi_y = jnp.where(sub == 7, zero, hi_y)
                faces.append((out_x * (edge_lo if k == 1 else edge_hi), lo_y, hi_y,
                              jnp.where(lane == 0, zero, lo_z), jnp.where(lane == 127, zero, hi_z)))
            for colour in (0, 1):
                lcoef[p, r, colour, 0] = in_x
                for k in range(5):
                    a, b = faces[colour][k], faces[1 - colour][k]
                    lcoef[p, r, colour, 1 + k] = jnp.where(par, a, b)
                lcoef[p, r, colour, 6] = 1.0 / jnp.where(par, diags[colour], diags[1 - colour])
        return 0

    lax.fori_loop(0, 18, build_low, 0)

    landed([copy for copy, (dw, dn) in zip(round2, LOW_SENDS) if abs(dw) < 4])
    source_shared = to_sibling(lambda planes: s2g.at[planes], (1, 2, 3))
    landed([copy for copy, (dw, dn) in zip(round2, LOW_SENDS) if abs(dw) == 4])
    source_shared += to_sibling(lambda planes: s2g.at[planes], (0, 4))
    everything += source_shared
    landed(source_shared)

    def load_low(q, _):
        p = q + 2 * core
        for r in range(4):
            a, b = s2g[2 * p, r], s2g[2 * p + 1, r]
            lsrc[0, p, r] = jnp.where(par, a, b)
            lsrc[1, p, r] = jnp.where(par, b, a)
            lv0[p, r] = lsrc[0, p, r] * lcoef[p, r, 0, 6]
        return 0

    lax.fori_loop(0, 18, load_low, 0, unroll=2)

    def low_half_sweep(colour, first, last):
        here, there = (lv0, lv1) if colour == 0 else (lv1, lv0)

        def body(q, _):
            first_pair = first + 2 * q + 2 * core
            seen = [[there[first_pair + k, r] for r in range(4)] for k in (-1, 0, 1, 2)]
            for k in (0, 1):
                p = first_pair + k
                before, other, after = seen[k:k + 3]
                downs = [down(value) for value in other]
                ups = [up(value) for value in other]
                for r in range(4):
                    coef = lambda which: lcoef[p, r, colour, which]
                    a, b = (before, after) if colour == 0 else (after, before)
                    total = lsrc[colour, p, r] + coef(0) * other[r] + coef(1) * jnp.where(par, a[r], b[r])
                    total += coef(2) * jnp.where(sub == 0, downs[r - 1], downs[r])
                    total += coef(3) * jnp.where(sub == 7, ups[(r + 1) % 4], ups[r])
                    total += coef(4) * left(other[r]) + coef(5) * right(other[r])
                    here[p, r] = total * coef(6)
            return 0

        steps = (last + 1 - first) // 2
        lax.fori_loop(0, steps, body, 0, unroll=2 if steps % 2 == 0 else 3 if steps % 3 == 0 else 1)

    for k in range(2, 13):
        low_half_sweep((k + 1) % 2, k // 2, 17 - k // 2)

    for i in range(12):
        v2t[i, 0:8, :] = zero
        v2t[i, 40:48, :] = zero
    for p in range(6):
        for r in range(4):
            a, b = lv0[6 + 2 * core + p, r], lv1[6 + 2 * core + p, r]
            v2t[2 * p, 8 + 8 * r:16 + 8 * r, :] = jnp.where(par, a, b)
            v2t[2 * p + 1, 8 + 8 * r:16 + 8 * r, :] = jnp.where(par, b, a)

    landed(mid_copies)

    def correct_mid(i, _):
        for j in range(4):
            coarse = v2t[i, pl.ds(8 * n + 4 + j // 2, 8, stride=2), :]
            for half in (0, 1):
                for t in range(2):
                    x = 2 * i + half
                    if (half + j + t) % 2 == 1:
                        mv1[x, j, t // 2] = vt[x, t, pl.ds(j, 8, stride=4), :] + coarse
        return 0

    lax.fori_loop(0, 12, correct_mid, 0)
    mid.half_sweep(0, 2, 20)
    mid.half_sweep(1, 3, 18)
    mid.half_sweep(0, 4, 16)
    mid.half_sweep(1, 5, 14)

    def spread_mid(q, _):
        for half in (0, 1):
            x = 5 + 2 * q + half
            get = mid.reader(x, 1 - half)
            for j in range(4):
                for t in range(2):
                    vp[x, t, pl.ds(j, 8, stride=4), :] = get(j, t)
        return 0

    lax.fori_loop(0, 7, spread_mid, 0)

    landed(fine_copies)
    unpack(tv, pyv, 0)
    unpack_fifth(tv, pyv5)
    unpack_corners((tv,), CORNER_V, pcv)

    def correct_fine(q, _):
        for j in range(3):
            for t in range(2):
                coarse = vp[q + 5, t, pl.ds(4 + j, 8, stride=3), :]
                for half in (0, 1):
                    x = 2 * q + half
                    for jj in (2 * j, 2 * j + 1):
                        for tt in (2 * t, 2 * t + 1):
                            if (half + jj + tt) % 2 == 1:
                                fv1[x, jj, tt // 2] = tv[x, tt, pl.ds(jj, 8, stride=6), :] + coarse
        return 0

    lax.fori_loop(0, 14, correct_fine, 0)
    fine.half_sweep(0, 2, 24)
    fine.half_sweep(1, 3, 22)
    fine.half_sweep(0, 4, 20)
    fine.half_sweep(1, 5, 18)

    for copy in round0:
        copy.wait_send()

    def result(k, x):
        staged, hbm = ((ts, hbm_v), (tc, hbm_r))[k]
        return pltpu.make_async_copy(staged.at[6 + x, :, pl.ds(8, 32)], hbm.at[x], out_sem.at[k, x])

    def finish(q, _):
        for half in (0, 1):
            x = 2 * q + half
            get = fine.reader(6 + x, half)
            for j in range(6):
                for t in range(4):
                    ts[6 + x, t, pl.ds(j, 8, stride=6), :] = get(j, t)
                    tc[6 + x, t, pl.ds(j, 8, stride=6), :] = fine.residual(6 + x, half, j, t, get)
            result(0, x).start()
            result(1, x).start()
        return 0

    def settle(x, _):
        result(0, x).wait()
        result(1, x).wait()
        return 0

    lax.fori_loop(0, 8, finish, 0)
    lax.fori_loop(0, 16, settle, 0)
    for copy in everything:
        copy.wait_send()


def join_kernel(v_ref, r_ref, out_v, out_r):
    def body(x, _):
        for tiles_ref, out in ((v_ref, out_v), (r_ref, out_r)):
            for r in range(4):
                tiles = [tiles_ref[x, t, 8 * r:8 * r + 8, :] for t in range(4)]
                for a, part in enumerate(join_lanes(tiles)):
                    out[x, 8 * r:8 * r + 8, 128 * a:128 * a + 128] = part
        return 0

    lax.fori_loop(0, v_ref.shape[0], body, 0)


def join(v, r):
    shape = jax.ShapeDtypeStruct((16, 32, 512), F32)
    tiles = pl.BlockSpec((8, 4, 32, 128), lambda i: (i, 0, 0, 0))
    whole = pl.BlockSpec((8, 32, 512), lambda i: (i, 0, 0))
    return pl.pallas_call(
        join_kernel, grid=(2,), out_shape=(shape, shape),
        in_specs=[tiles] * 2, out_specs=(whole, whole),
        compiler_params=pltpu.CompilerParams(vmem_limit_bytes=60 * 2**20),
    )(v, r)


N_COPIES = 14 + 8 + 8 + 3 + 4 + 8 + 10 + 5 + 17 + 8 + 5


def vmem(*shape):
    return pltpu.VMEM(shape, F32)


def v_cycle(rhs, cf, cm, cl):
    hbm = pl.BlockSpec(memory_space=pl.ANY)
    shape = jax.ShapeDtypeStruct((16, 4, 32, 128), F32)
    fine_t = (28, 4, 48, 128)
    fine_a = (28, 6, 4, 8, 128)
    mid_t = (24, 2, 32, 128)
    mid_a = (24, 4, 2, 8, 128)
    scratch = [
        vmem(*rhs.shape), vmem(*cf.shape), vmem(*cm.shape), vmem(*cl.shape),
        pltpu.SemaphoreType.DMA((5,)), pltpu.SemaphoreType.DMA((2, 16)),
        vmem(*fine_t), vmem(*fine_t), vmem(*fine_t), vmem(*fine_t),
        vmem(2, 3, 8, 4, 8, 128), vmem(2, 4, 16, 128), vmem(4, 4, 16, 128), vmem(4, 4, 8, 128),
        vmem(2, 3, 8, 4, 8, 128), vmem(2, 4, 16, 128), vmem(4, 4, 16, 128), vmem(4, 4, 8, 128),
        vmem(*fine_a), vmem(*fine_a), vmem(28, 7, 4, 8, 128), vmem(28, 6, 5, 8, 128),
        vmem(*fine_a), vmem(*fine_a), vmem(*fine_a), vmem(28, 6, 2, 8, 128), vmem(28, 6, 2, 8, 128),
        vmem(2, *mid_t), vmem(*mid_t), vmem(*mid_t), vmem(*mid_t),
        vmem(*mid_a), vmem(*mid_a), vmem(24, 5, 2, 8, 128), vmem(24, 4, 3, 8, 128),
        vmem(*mid_a), vmem(*mid_a), vmem(*mid_a), vmem(24, 4, 1, 8, 128), vmem(24, 4, 1, 8, 128),
        vmem(8, 2, 32, 128), vmem(4, 16, 128),
        vmem(2, 40, 4, 8, 128), vmem(4, 8, 128), vmem(40, 4, 8, 128), vmem(42, 4, 8, 128),
        vmem(20, 4, 2, 7, 8, 128), vmem(2, 20, 4, 8, 128), vmem(20, 4, 8, 128), vmem(20, 4, 8, 128), vmem(12, 48, 128),
        vmem(2, 1, 8, 4, 8, 128), vmem(2, 4, 16, 128), vmem(4, 4, 16, 128),
        vmem(2, 1, 8, 4, 8, 128), vmem(2, 4, 16, 128), vmem(4, 4, 16, 128),
        pltpu.SemaphoreType.DMA((N_COPIES,)), pltpu.SemaphoreType.DMA((N_COPIES,)),
    ]
    return pl.pallas_call(
        kernel,
        out_shape=(shape, shape),
        in_specs=[hbm] * 4,
        out_specs=(hbm, hbm),
        scratch_shapes=scratch,
        compiler_params=pltpu.CompilerParams(
            collective_id=0, has_side_effects=True, vmem_limit_bytes=60 * 2**20),
    )(rhs, cf, cm, cl)


def shift_kernel(k, cm, cl, out_m, out_l, send, recv):
    w, n = lax.axis_index("wide"), lax.axis_index("narrow")
    barrier = pltpu.get_barrier_semaphore()
    pl.semaphore_signal(barrier, inc=1, device_id=(lax.rem(w + k, NW), n), device_id_type=MESH)
    pl.semaphore_wait(barrier, 1)
    copies = [
        pltpu.make_async_remote_copy(
            src_ref=src, dst_ref=dst, send_sem=send.at[i], recv_sem=recv.at[i],
            device_id=(lax.rem(w + (NW - k), NW), n), device_id_type=MESH)
        for i, (src, dst) in enumerate(((cm, out_m), (cl, out_l)))]
    for copy in copies:
        copy.start()
    for copy in copies:
        copy.wait()


def on_device(rhs, cf, cm, cl, offset):
    def moved(k):
        return lambda a, b: pl.pallas_call(
            functools.partial(shift_kernel, k),
            out_shape=(jax.ShapeDtypeStruct(a.shape, F32), jax.ShapeDtypeStruct(b.shape, F32)),
            in_specs=[pl.BlockSpec(memory_space=pl.ANY)] * 2,
            out_specs=(pl.BlockSpec(memory_space=pl.ANY),) * 2,
            scratch_shapes=[pltpu.SemaphoreType.DMA((2,)), pltpu.SemaphoreType.DMA((2,))],
            compiler_params=pltpu.CompilerParams(collective_id=k, has_side_effects=True),
        )(a, b)

    cm, cl = lax.switch(offset[0] - 1, [moved(k) for k in range(1, NW)], cm, cl)
    return join(*v_cycle(rhs, cf, cm, cl))


def solution(mesh):
    return jax.shard_map(
        on_device,
        mesh=mesh,
        in_specs=(
            P("wide", "narrow", None),
            P(None, "wide", "narrow", None),
            P(None, "wide", "narrow", None),
            P(None, "wide", "narrow", None),
            P(),
        ),
        out_specs=(P("wide", "narrow", None), P("wide", "narrow", None)),
        check_vma=False,
    )
```

```python
import functools

import jax
import jax.numpy as jnp
from jax import lax
from jax.experimental import pallas as pl
from jax.experimental.pallas import tpu as pltpu
from jax.sharding import PartitionSpec as P

MESH = pl.DeviceIdType.MESH
F32 = jnp.float32
NW, NN = 32, 4
LOW_SENDS = [(dw, dn) for dw in (-4, 4, -2, 2, 0) for dn in (-1, 0, 1, 2)
             if (dw, dn) not in ((0, 0), (-4, 2), (4, 2))]
CORNERS = [(dw, dn) for dw in (-1, 1) for dn in (-1, 1)]
SIDES = [(-1, 0), (1, 0), (0, -1), (0, 1)]
GREETED = SIDES + CORNERS + [(-2, 0), (2, 0), (-4, 0), (4, 0), (0, 2)]
NEAR = [(dx, dy) for dx in range(1, 5) for dy in range(1, 5)]
CORNER_BC = [(f, dx, dy) for f in (0, 1) for dx, dy in NEAR if dx + dy <= 5 - f]
CORNER_S = [(0, dx, dy) for dx, dy in NEAR if dx + dy <= 4]
CORNER_V = [(0, dx, dy) for dx, dy in NEAR if dx + dy <= 5]


def iota(axis):
    return lax.broadcasted_iota(jnp.int32, (8, 128), axis)


def take(x, index):
    return jnp.take_along_axis(x, index, axis=1, mode="promise_in_bounds")


def swap(first, second, bit):
    low = iota(1) & bit == 0
    return (jnp.where(low, first, pltpu.roll(second, bit, 1)),
            jnp.where(low, pltpu.roll(first, 128 - bit, 1), second))


def split_lanes(parts):
    a, b = swap(parts[0], parts[1], 1)
    c, d = swap(parts[2], parts[3], 1)
    (a, c), (b, d) = swap(a, c, 2), swap(b, d, 2)
    return [a, b, c, d]


def join_lanes(tiles):
    a, b, c, d = tiles
    (a, c), (b, d) = swap(a, c, 2), swap(b, d, 2)
    a, b = swap(a, b, 1)
    c, d = swap(c, d, 1)
    return [a, b, c, d]


def place_index():
    lane = iota(1)
    return 32 * (lane % 4) + lane // 4


def down(x):
    return pltpu.roll(x, 1, 0)


def up(x):
    return pltpu.roll(x, 7, 0)


def left(x):
    return jnp.where(iota(1) < 4, pltpu.roll(x, 5, 1), pltpu.roll(x, 4, 1))


def right(x):
    return jnp.where(iota(1) >= 124, pltpu.roll(x, 123, 1), pltpu.roll(x, 124, 1))


class Level:
    def __init__(self, J, T, h, fx, fy, fz, rinv, diag, src, v):
        self.J, self.T = J, T
        self.h, self.fx, self.fy, self.fz = h, fx, fy, fz
        self.rinv, self.diag, self.src, self.v = rinv, diag, src, v

    def unroll(self, steps):
        return 1 if self.T == 4 else 2 if steps % 2 == 0 else 3 if steps % 3 == 0 else 1

    def cells(self, parity):
        return [(j, t) for j in range(self.J) for t in range(self.T) if (j + t) % 2 == parity]

    def setup(self, b_of, c_of, first, count, plane_lo, plane_hi, row_lo, row_hi):
        J, T = self.J, self.T
        lane = iota(1)
        row = J * iota(0)
        zero = jnp.zeros((8, 128), F32)

        def fill(x, _):
            scale = jnp.where((x >= plane_lo) & (x < plane_hi), 0.5, 0.0).astype(F32)
            for j in range(J):
                inside = (row + j >= row_lo) & (row + j < row_hi)
                for t in range(T):
                    self.h[x, j, t] = jnp.where(inside, b_of(x, j, t) * scale, zero)
            return 0

        lax.fori_loop(first - 1, first + count + 1, fill, 0)

        def open_face(x):
            return jnp.where((x == plane_lo) | (x == plane_hi), 0.0, 1.0).astype(F32)

        for j in range(J):
            for t in range(T):
                self.fx[first, j, t] = (self.h[first - 1, j, t] + self.h[first, j, t]) * open_face(first)

        def build(x, _):
            h = {(j, t): self.h[x, j, t] for j in range(J) for t in range(T)}
            edge_hi = open_face(x + 1)
            for t in range(T):
                real_y = [h[j, t] + (h[j - 1, t] if j else down(h[J - 1, t])) for j in range(J)]
                real_y.append(up(real_y[0]))
                for j in range(J + 1):
                    closed = (row + j == row_lo) | (row + j == row_hi)
                    self.fy[x, j, t] = jnp.where(closed, zero, real_y[j])
                for j in range(J):
                    here = h[j, t]
                    lo_x = self.h[x - 1, j, t] + here
                    hi_x = self.h[x + 1, j, t] + here
                    self.fx[x + 1, j, t] = hi_x * edge_hi
                    if t:
                        lo_z = here + h[j, t - 1]
                        self.fz[x, j, t] = lo_z
                    else:
                        beside = jnp.where(lane == 0, zero, left(h[j, T - 1]))
                        lo_z = here + beside
                        self.fz[x, j, t] = jnp.where(lane == 0, zero, lo_z)
                    if t < T - 1:
                        hi_z = here + h[j, t + 1]
                    else:
                        beside = jnp.where(lane == 127, zero, right(h[j, 0]))
                        hi_z = here + beside
                        self.fz[x, j, T] = jnp.where(lane == 127, zero, hi_z)
                    diag = lo_x + hi_x + real_y[j] + real_y[j + 1] + lo_z + hi_z + c_of(x, j, t)
                    self.diag[x, j, t] = diag
                    self.rinv[x, j, t] = 1.0 / diag
            return 0

        lax.fori_loop(first, first + count, build, 0, unroll=self.unroll(count))

    def pulled(self, x, j, t, colour, get):
        J, T, other = self.J, self.T, self.v[1 - colour]
        total = self.fx[x, j, t] * other[x - 1, j, t // 2] + self.fx[x + 1, j, t] * other[x + 1, j, t // 2]
        total += self.fy[x, j, t] * (get(j - 1, t) if j else down(get(J - 1, t)))
        total += self.fy[x, j + 1, t] * (get(j + 1, t) if j < J - 1 else up(get(0, t)))
        total += self.fz[x, j, t] * (get(j, t - 1) if t else left(get(j, T - 1)))
        total += self.fz[x, j, t + 1] * (get(j, t + 1) if t < T - 1 else right(get(j, 0)))
        return total

    def reader(self, x, parity):
        seen = {}

        def get(j, t):
            if (j, t) not in seen:
                seen[j, t] = self.v[(parity + j + t) % 2][x, j, t // 2]
            return seen[j, t]

        return get

    def start(self, first, count):
        def body(i, _):
            for half in (0, 1):
                x = first + 2 * i + half
                for j, t in self.cells((first + half) % 2):
                    self.v[0][x, j, t // 2] = self.src[x, j, t] * self.rinv[x, j, t]
            return 0

        lax.fori_loop(0, count // 2, body, 0, unroll=self.unroll(count // 2))

    def half_sweep(self, colour, first, count):
        def body(i, _):
            for half in (0, 1):
                x = first + 2 * i + half
                get = self.reader(x, (first + half) % 2)
                for j, t in self.cells((first + half + colour) % 2):
                    total = self.src[x, j, t] + self.pulled(x, j, t, colour, get)
                    self.v[colour][x, j, t // 2] = total * self.rinv[x, j, t]
            return 0

        lax.fori_loop(0, count // 2, body, 0, unroll=self.unroll(count // 2))

    def residual(self, x, parity, j, t, get):
        pulled = self.pulled(x, j, t, (parity + j + t) % 2, get)
        return self.src[x, j, t] - (self.diag[x, j, t] * get(j, t) - pulled)

    def restrict_pair(self, x):
        sums = {}
        for half in (0, 1):
            get = self.reader(x + half, half)
            for j in range(self.J):
                for t in range(self.T):
                    value = self.residual(x + half, half, j, t, get)
                    key = (j // 2, t // 2)
                    sums[key] = sums[key] + value if key in sums else value
        return {key: 0.5 * value for key, value in sums.items()}


def kernel(rhs_hbm, cf_hbm, cm_hbm, cl_hbm, hbm_v, hbm_r,
           rhs, cf, cm, cl, in_sem, out_sem,
           tb, tc, ts, tv, pk, pk5, pkc, pkcs, py, py5, pc, pcs,
           fh, ffx, ffy, ffz, frinv, fdiag, fsrc, fv0, fv1,
           mt, st, vt, vp, mh, mfx, mfy, mfz, mrinv, mdiag, msrc, mv0, mv1, mstage, lstage,
           lc, s2own, s2g, lh, lcoef, lsrc, lv0, lv1, v2t,
           pkv, pkv5, pkvc, pyv, pyv5, pcv,
           send, recv):
    w = lax.axis_index("wide")
    n = lax.axis_index("narrow")
    core = lax.rem(w, 2)

    def device(dw, dn):
        return (lax.rem(w + (dw + NW), NW), lax.rem(n + (dn + NN), NN))

    loads = [pltpu.make_async_copy(cf_hbm.at[0], cf.at[0], in_sem.at[0]),
             pltpu.make_async_copy(cf_hbm.at[1], cf.at[1], in_sem.at[1]),
             pltpu.make_async_copy(rhs_hbm, rhs, in_sem.at[2]),
             pltpu.make_async_copy(cm_hbm, cm, in_sem.at[3]),
             pltpu.make_async_copy(cl_hbm, cl, in_sem.at[4])]
    for load in loads:
        load.start()
    ones, zeros = jnp.ones((8, 128), F32), jnp.zeros((8, 128), F32)
    for x in (*range(8), *range(32, 40)):
        for r in range(4):
            lc[0, x, r] = ones
            lc[1, x, r] = ones
            s2g[x, r] = zeros
    barrier = pltpu.get_barrier_semaphore()
    for dw, dn in GREETED:
        pl.semaphore_signal(barrier, inc=1, device_id=device(dw, dn), device_id_type=MESH)

    count = [0]

    def remote(src, dst, dw, dn):
        k = count[0]
        count[0] += 1
        copy = pltpu.make_async_remote_copy(
            src_ref=src, dst_ref=dst, send_sem=send.at[k], recv_sem=recv.at[k],
            device_id=device(dw, dn), device_id_type=MESH)
        copy.start()
        return copy

    def landed(copies):
        for copy in copies:
            copy.wait_recv()

    everything = []

    def to_split(read, target):
        def body(x, _):
            for r in range(4):
                parts = [read(x, r, a) for a in range(4)]
                for t, tile in enumerate(split_lanes(parts)):
                    target[6 + x, t, 8 + 8 * r:16 + 8 * r, :] = tile
            return 0

        lax.fori_loop(0, 16, body, 0)

    def pack(field, packed, which):
        def body(p, _):
            for t in range(4):
                for half in (0, 1):
                    x = 6 + 2 * p + half
                    packed[0, which, p, t, 4 * half:4 * half + 4, :] = field[x, t, 8:12, :]
                    packed[1, which, p, t, 4 * half:4 * half + 4, :] = field[x, t, 36:40, :]
            return 0

        lax.fori_loop(0, 8, body, 0)

    def pack_fifth(field, packed):
        def body(x, _):
            for t in range(4):
                packed[0, t, pl.ds(x, 1), :] = field[6 + x, t, 12:13, :]
                packed[1, t, pl.ds(x, 1), :] = field[6 + x, t, 35:36, :]
            return 0

        lax.fori_loop(0, 16, body, 0)

    def send_planes(field, layers):
        own = pl.ds(8, 32)
        return [
            remote(field.at[pl.ds(6, layers), :, own], field.at[pl.ds(22, layers), :, own], -1, 0),
            remote(field.at[pl.ds(22 - layers, layers), :, own], field.at[pl.ds(6 - layers, layers), :, own], 1, 0),
        ]

    def pack_corners(fields, rows, packed):
        def body(corner, _):
            cw, cn = corner // 2, corner % 2
            for r, (f, dx, dy) in enumerate(rows):
                x = 5 + dx + cw * (17 - 2 * dx)
                y = 7 + dy + cn * (33 - 2 * dy)
                for t in range(4):
                    packed[corner, t, r:r + 1, :] = fields[f][x, t, pl.ds(y, 1), :]
            return 0

        lax.fori_loop(0, 4, body, 0)

    def unpack_corners(fields, rows, got):
        def body(corner, _):
            cw, cn = corner // 2, corner % 2
            for r, (f, dx, dy) in enumerate(rows):
                x = 6 - dx + cw * (15 + 2 * dx)
                y = 8 - dy + cn * (31 + 2 * dy)
                for t in range(4):
                    fields[f][x, t, pl.ds(y, 1), :] = got[corner, t, r:r + 1, :]
            return 0

        lax.fori_loop(0, 4, body, 0)

    def send_corners(corner, got_corner):
        copies = []
        for dw, dn in CORNERS:
            here = (dw + 1) + (dn + 1) // 2
            copies.append(remote(corner.at[here], got_corner.at[3 - here], dw, dn))
        return copies

    def send_rows(packed, got):
        return [remote(packed.at[0], got.at[1], 0, -1), remote(packed.at[1], got.at[0], 0, 1)]

    def unpack(field, got, which):
        def place(x, t, half, lower, upper):
            field[x, t, 4:8, :] = lower[4 * half:4 * half + 4]
            field[x, t, 40:44, :] = upper[4 * half:4 * half + 4]

        def body(p, _):
            for t in range(4):
                lower, upper = got[0, which, p, t], got[1, which, p, t]
                for half in (0, 1):
                    place(6 + 2 * p + half, t, half, lower, upper)
            return 0

        lax.fori_loop(0, 8, body, 0)

    def unpack_fifth(field, got5):
        def body(x, _):
            for t in range(4):
                field[6 + x, t, 3:4, :] = got5[0, t, pl.ds(x, 1), :]
                field[6 + x, t, 44:45, :] = got5[1, t, pl.ds(x, 1), :]
            return 0

        lax.fori_loop(0, 16, body, 0)

    loads[0].wait()
    to_split(lambda x, r, a: cf[0, x, 8 * r:8 * r + 8, 128 * a:128 * a + 128], tb)
    pl.semaphore_wait(barrier, len(GREETED))
    round0_coef = send_planes(tb, 5)
    pack(tb, pk, 2)
    round0_coef += send_rows(pk.at[:, 2], py.at[:, 2])
    pack_fifth(tb, pk5)
    round0_coef += send_rows(pk5, py5)
    loads[1].wait()
    to_split(lambda x, r, a: cf[1, x, 8 * r:8 * r + 8, 128 * a:128 * a + 128], tc)
    round0_coef += send_planes(tc, 4)
    pack(tc, pk, 1)
    round0_coef += send_rows(pk.at[:, 1], py.at[:, 1])
    pack_corners((tb, tc), CORNER_BC, pkc)
    round0_coef += send_corners(pkc, pc)
    loads[4].wait()
    for which in (0, 1):
        for x in range(4):
            lc[which, 16 + 4 * core + x, n] = cl[which, x]
    coef_rows = []
    for dn in (1, 3, 2):
        mine = lc.at[:, pl.ds(16 + 4 * core, 4), n]
        coef_rows.append(remote(mine, mine, 0, dn))
    everything += coef_rows

    loads[2].wait()
    to_split(lambda x, r, a: rhs[x, 8 * r:8 * r + 8, 128 * a:128 * a + 128], ts)
    round0_src = send_planes(ts, 4)
    pack(ts, pk, 0)
    round0_src += send_rows(pk.at[:, 0], py.at[:, 0])
    pack_corners((ts,), CORNER_S, pkcs)
    round0_src += send_corners(pkcs, pcs)
    round0 = round0_coef + round0_src

    place = place_index()

    def split_mid(x, _):
        for which in (0, 1):
            for r in range(2):
                low, high = [cm[which, x, 8 * r:8 * r + 8, 128 * a:128 * a + 128] for a in range(2)]
                for t in range(2):
                    index = (2 * place + t) % 128
                    tile = jnp.where(place < 64, take(low, index), take(high, index))
                    mt[which, 8 + x, t, 8 + 8 * r:16 + 8 * r, :] = tile
        return 0

    loads[3].wait()
    lax.fori_loop(0, 8, split_mid, 0)

    def mid_slices(dw, dn, depth=8):
        depth = 8 if dw == 0 else depth
        planes = pl.ds(16 - depth if dw > 0 else 8, depth)
        planes_there = pl.ds(8 if dw == 0 else 16 if dw < 0 else 8 - depth, depth)
        rows = pl.ds(8, 16) if dn == 0 else pl.ds(8 if dn < 0 else 16, 8)
        rows_there = pl.ds(8, 16) if dn == 0 else pl.ds(24 if dn < 0 else 0, 8)
        return planes, rows, planes_there, rows_there

    def send_mid(field, depth):
        copies = []
        for dw, dn in SIDES + CORNERS:
            planes, rows, planes_there, rows_there = mid_slices(dw, dn, depth)
            copies.append(remote(field.at[planes, :, rows], field.at[planes_there, :, rows_there], dw, dn))
        return copies

    def send_low(src, dst_of):
        return [remote(src, dst_of(4 - dw + core), dw, dn) for dw, dn in LOW_SENDS]

    landed(round0_coef)
    mid_coef_copies = []
    for dw, dn in SIDES + CORNERS:
        planes, rows, planes_there, rows_there = mid_slices(dw, dn, 7)
        mid_coef_copies.append(remote(mt.at[:, planes, :, rows], mt.at[:, planes_there, :, rows_there], dw, dn))
    everything += mid_coef_copies

    landed(coef_rows)

    def send_low_coef(dw, rows):
        src = lc.at[:, pl.ds(16 + 4 * core, 4), rows]
        return remote(src, lc.at[:, pl.ds(4 * (4 - dw + core), 4), rows], dw, 0)

    low_coef_near = [send_low_coef(dw, pl.ds(0, 4)) for dw in (-2, 2)]
    everything += low_coef_near
    unpack(tb, py, 2)
    unpack(tc, py, 1)
    unpack_fifth(tb, py5)
    unpack_corners((tb, tc), CORNER_BC, pc)

    row_lo = lambda rows: jnp.where(n == 0, rows, 0)
    row_hi = lambda edge, last: jnp.where(n == NN - 1, edge, last)
    first_box, last_box = w == 0, w == NW - 1

    fine = Level(6, 4, fh, ffx, ffy, ffz, frinv, fdiag, fsrc, (fv0, fv1))
    fine.setup(
        lambda x, j, t: tb[x, t, pl.ds(j, 8, stride=6), :],
        lambda x, j, t: tc[x, t, pl.ds(j, 8, stride=6), :],
        2, 24,
        jnp.where(first_box, 6, -1), jnp.where(last_box, 22, 99),
        row_lo(8), row_hi(40, 48))

    landed(round0_src)

    unpack(ts, py, 0)
    unpack_corners((ts,), CORNER_S, pcs)

    def load_fine(x, _):
        for j in range(6):
            for t in range(4):
                fsrc[x, j, t] = ts[x, t, pl.ds(j, 8, stride=6), :]
        return 0

    lax.fori_loop(2, 26, load_fine, 0)
    fine.start(2, 24)
    fine.half_sweep(1, 3, 22)

    fine.half_sweep(0, 4, 20)
    fine.half_sweep(1, 5, 18)

    def restrict_fine(i, _):
        for (j, t), value in fine.restrict_pair(6 + 2 * i).items():
            mstage[i, t, pl.ds(4 + j, 8, stride=3), :] = value
        for t in range(2):
            st[8 + i, t, 8:24, :] = mstage[i, t, 8:24, :]
        return 0

    lax.fori_loop(0, 8, restrict_fine, 0)

    round1 = send_mid(st, 6)
    low_coef_far = [send_low_coef(dw, pl.ds(n // 2, 3)) for dw in (-4, 4)]
    everything += round1 + low_coef_far

    landed(mid_coef_copies)
    mid = Level(4, 2, mh, mfx, mfy, mfz, mrinv, mdiag, msrc, (mv0, mv1))
    mid.setup(
        lambda x, j, t: mt[0, x, t, pl.ds(j, 8, stride=4), :],
        lambda x, j, t: mt[1, x, t, pl.ds(j, 8, stride=4), :],
        1, 22,
        jnp.where(first_box, 8, -1), jnp.where(last_box, 16, 99),
        row_lo(8), row_hi(24, 32))

    landed(round1)

    def load_mid(x, _):
        for j in range(4):
            for t in range(2):
                msrc[x, j, t] = st[x, t, pl.ds(j, 8, stride=4), :]
        return 0

    lax.fori_loop(2, 22, load_mid, 0)
    mid.start(4, 16)
    mid.half_sweep(1, 5, 14)
    mid.half_sweep(0, 6, 12)
    mid.half_sweep(1, 7, 10)

    natural = 4 * (iota(1) % 32) + iota(1) // 32

    def restrict_mid(i, _):
        for (j, t), value in mid.restrict_pair(8 + 2 * i).items():
            lstage[i, pl.ds(j, 8, stride=2), :] = value
        value = take(lstage[i, 4:12, :], natural)
        s2own[i] = value
        s2g[16 + 4 * core + i, n] = value
        return 0

    lax.fori_loop(0, 4, restrict_mid, 0)

    def to_sibling(refs_of, boxes):
        copies = []
        for box in boxes:
            part = refs_of(pl.ds(8 * box + 4 * core, 4))
            k = count[0]
            count[0] += 1
            copy = pltpu.make_async_remote_copy(
                src_ref=part, dst_ref=part, send_sem=send.at[k], recv_sem=recv.at[k],
                device_id=(w + 1 - 2 * core, n), device_id_type=MESH)
            copy.start()
            copies.append(copy)
        return copies

    round2 = send_low(s2own, lambda slot: s2g.at[pl.ds(4 * slot, 4), n])
    everything += round2

    def store_mid(q, _):
        for half in (0, 1):
            x = 2 * q + half
            get = mid.reader(8 + x, half)
            for j in range(4):
                for t in range(2):
                    mstage[x, t, pl.ds(j, 8, stride=4), :] = get(j, t)
            for t in range(2):
                vt[8 + x, t, 8:24, :] = mstage[x, t, 8:24, :]
        return 0

    lax.fori_loop(0, 4, store_mid, 0)
    landed(low_coef_near + low_coef_far)
    low_coef_shared = to_sibling(lambda planes: lc.at[:, planes], range(5))
    everything += low_coef_shared

    mid_copies = send_mid(vt, 8)
    everything += mid_copies

    def store_fine(q, _):
        for half in (0, 1):
            x = 6 + 2 * q + half
            get = fine.reader(x, half)
            for j in range(6):
                for t in range(4):
                    tv[x, t, pl.ds(j, 8, stride=6), :] = get(j, t)
        return 0

    lax.fori_loop(0, 8, store_fine, 0)
    pack(tv, pkv, 0)
    pack_fifth(tv, pkv5)
    pack_corners((tv,), CORNER_V, pkvc)
    fine_copies = send_planes(tv, 5) + send_rows(pkv.at[:, 0], pyv.at[:, 0]) + send_rows(pkv5, pyv5)
    fine_copies += send_corners(pkvc, pcv)
    everything += fine_copies

    landed(low_coef_shared)
    lane, sub = iota(1), iota(0)
    par = (lane + sub) % 2 == 0
    zero = jnp.zeros((8, 128), F32)
    low_lo = 16 - 4 * (w - core)
    low_hi = low_lo + 4 * NW

    for r in range(4):
        lh[0, r] = zero
        lh[41, r] = zero

    def fill_low(i, _):
        scale = jnp.where((i >= low_lo) & (i < low_hi), 0.5, 0.0).astype(F32)
        for r in range(4):
            lh[1 + i, r] = lc[0, i, r] * scale
        return 0

    lax.fori_loop(0, 40, fill_low, 0, unroll=4)

    def open_low(i):
        return jnp.where((i == low_lo) | (i == low_hi), 0.0, 1.0).astype(F32)

    def build_low(q, _):
        p = q + 2 * core
        i = 2 * p
        edge_lo, edge_hi = open_low(i), open_low(i + 2)
        h = [[lh[i + k, r] for r in range(4)] for k in range(4)]
        for r in range(4):
            lo_x = h[0][r] + h[1][r]
            in_x = h[1][r] + h[2][r]
            hi_x = h[2][r] + h[3][r]
            faces, diags = [], []
            for k in (1, 2):
                here = h[k][r]
                below = jnp.where(sub == 0, down(h[k][r - 1]) if r else zero, down(here))
                above = jnp.where(sub == 7, up(h[k][r + 1]) if r < 3 else zero, up(here))
                lo_y, hi_y = here + below, here + above
                lo_z = here + jnp.where(lane == 0, zero, pltpu.roll(here, 1, 1))
                hi_z = here + jnp.where(lane == 127, zero, pltpu.roll(here, 127, 1))
                out_x = lo_x if k == 1 else hi_x
                diags.append(in_x + out_x + lo_y + hi_y + lo_z + hi_z + lc[1, i + k - 1, r])
                if r == 0:
                    lo_y = jnp.where(sub == 0, zero, lo_y)
                if r == 3:
                    hi_y = jnp.where(sub == 7, zero, hi_y)
                faces.append((out_x * (edge_lo if k == 1 else edge_hi), lo_y, hi_y,
                              jnp.where(lane == 0, zero, lo_z), jnp.where(lane == 127, zero, hi_z)))
            for colour in (0, 1):
                lcoef[p, r, colour, 0] = in_x
                for k in range(5):
                    a, b = faces[colour][k], faces[1 - colour][k]
                    lcoef[p, r, colour, 1 + k] = jnp.where(par, a, b)
                lcoef[p, r, colour, 6] = 1.0 / jnp.where(par, diags[colour], diags[1 - colour])
        return 0

    lax.fori_loop(0, 18, build_low, 0)

    landed([copy for copy, (dw, dn) in zip(round2, LOW_SENDS) if abs(dw) < 4])
    source_shared = to_sibling(lambda planes: s2g.at[planes], (1, 2, 3))
    landed([copy for copy, (dw, dn) in zip(round2, LOW_SENDS) if abs(dw) == 4])
    source_shared += to_sibling(lambda planes: s2g.at[planes], (0, 4))
    everything += source_shared
    landed(source_shared)

    def load_low(q, _):
        p = q + 2 * core
        for r in range(4):
            a, b = s2g[2 * p, r], s2g[2 * p + 1, r]
            lsrc[0, p, r] = jnp.where(par, a, b)
            lsrc[1, p, r] = jnp.where(par, b, a)
            lv0[p, r] = lsrc[0, p, r] * lcoef[p, r, 0, 6]
        return 0

    lax.fori_loop(0, 18, load_low, 0, unroll=2)

    def low_half_sweep(colour, first, last):
        here, there = (lv0, lv1) if colour == 0 else (lv1, lv0)

        def body(q, _):
            first_pair = first + 2 * q + 2 * core
            seen = [[there[first_pair + k, r] for r in range(4)] for k in (-1, 0, 1, 2)]
            for k in (0, 1):
                p = first_pair + k
                before, other, after = seen[k:k + 3]
                downs = [down(value) for value in other]
                ups = [up(value) for value in other]
                for r in range(4):
                    coef = lambda which: lcoef[p, r, colour, which]
                    a, b = (before, after) if colour == 0 else (after, before)
                    total = lsrc[colour, p, r] + coef(0) * other[r] + coef(1) * jnp.where(par, a[r], b[r])
                    total += coef(2) * jnp.where(sub == 0, downs[r - 1], downs[r])
                    total += coef(3) * jnp.where(sub == 7, ups[(r + 1) % 4], ups[r])
                    total += coef(4) * pltpu.roll(other[r], 1, 1) + coef(5) * pltpu.roll(other[r], 127, 1)
                    here[p, r] = total * coef(6)
            return 0

        steps = (last + 1 - first) // 2
        lax.fori_loop(0, steps, body, 0, unroll=2 if steps % 2 == 0 else 3 if steps % 3 == 0 else 1)

    for k in range(2, 13):
        low_half_sweep((k + 1) % 2, k // 2, 17 - k // 2)

    for i in range(12):
        v2t[i, 0:8, :] = zero
        v2t[i, 40:48, :] = zero
    for p in range(6):
        for r in range(4):
            a, b = lv0[6 + 2 * core + p, r], lv1[6 + 2 * core + p, r]
            v2t[2 * p, 8 + 8 * r:16 + 8 * r, :] = jnp.where(par, a, b)
            v2t[2 * p + 1, 8 + 8 * r:16 + 8 * r, :] = jnp.where(par, b, a)

    landed(mid_copies)

    def correct_mid(i, _):
        for j in (0, 2):
            coarse = take(v2t[i, pl.ds(8 * n + 4 + j // 2, 8, stride=2), :], place)
            for half in (0, 1):
                for jj in (j, j + 1):
                    for t in range(2):
                        x = 2 * i + half
                        if (half + jj + t) % 2 == 1:
                            mv1[x, jj, t // 2] = vt[x, t, pl.ds(jj, 8, stride=4), :] + coarse
        return 0

    lax.fori_loop(0, 12, correct_mid, 0)
    mid.half_sweep(0, 2, 20)
    mid.half_sweep(1, 3, 18)
    mid.half_sweep(0, 4, 16)
    mid.half_sweep(1, 5, 14)

    def spread_mid(q, _):
        for half in (0, 1):
            x = 5 + 2 * q + half
            get = mid.reader(x, 1 - half)
            for j in range(4):
                for t in range(2):
                    vp[x, t, pl.ds(j, 8, stride=4), :] = get(j, t)
        return 0

    lax.fori_loop(0, 7, spread_mid, 0)

    landed(fine_copies)
    unpack(tv, pyv, 0)
    unpack_fifth(tv, pyv5)
    unpack_corners((tv,), CORNER_V, pcv)

    def correct_fine(q, _):
        for j in range(3):
            for t in range(2):
                coarse = vp[q + 5, t, pl.ds(4 + j, 8, stride=3), :]
                for half in (0, 1):
                    x = 2 * q + half
                    for jj in (2 * j, 2 * j + 1):
                        for tt in (2 * t, 2 * t + 1):
                            if (half + jj + tt) % 2 == 1:
                                fv1[x, jj, tt // 2] = tv[x, tt, pl.ds(jj, 8, stride=6), :] + coarse
        return 0

    lax.fori_loop(0, 14, correct_fine, 0)
    fine.half_sweep(0, 2, 24)
    fine.half_sweep(1, 3, 22)
    fine.half_sweep(0, 4, 20)
    fine.half_sweep(1, 5, 18)

    for copy in round0:
        copy.wait_send()

    def result(k, x):
        staged, hbm = ((ts, hbm_v), (tc, hbm_r))[k]
        return pltpu.make_async_copy(staged.at[6 + x, :, pl.ds(8, 32)], hbm.at[x], out_sem.at[k, x])

    def finish(q, _):
        for half in (0, 1):
            x = 2 * q + half
            get = fine.reader(6 + x, half)
            for j in range(6):
                for t in range(4):
                    ts[6 + x, t, pl.ds(j, 8, stride=6), :] = get(j, t)
                    tc[6 + x, t, pl.ds(j, 8, stride=6), :] = fine.residual(6 + x, half, j, t, get)
            result(0, x).start()
            result(1, x).start()
        return 0

    def settle(x, _):
        result(0, x).wait()
        result(1, x).wait()
        return 0

    lax.fori_loop(0, 8, finish, 0)
    lax.fori_loop(0, 16, settle, 0)
    for copy in everything:
        copy.wait_send()


def join_kernel(v_ref, r_ref, out_v, out_r):
    def body(x, _):
        for tiles_ref, out in ((v_ref, out_v), (r_ref, out_r)):
            for r in range(4):
                tiles = [tiles_ref[x, t, 8 * r:8 * r + 8, :] for t in range(4)]
                for a, part in enumerate(join_lanes(tiles)):
                    out[x, 8 * r:8 * r + 8, 128 * a:128 * a + 128] = part
        return 0

    lax.fori_loop(0, v_ref.shape[0], body, 0)


def join(v, r):
    shape = jax.ShapeDtypeStruct((16, 32, 512), F32)
    tiles = pl.BlockSpec((8, 4, 32, 128), lambda i: (i, 0, 0, 0))
    whole = pl.BlockSpec((8, 32, 512), lambda i: (i, 0, 0))
    return pl.pallas_call(
        join_kernel, grid=(2,), out_shape=(shape, shape),
        in_specs=[tiles] * 2, out_specs=(whole, whole),
        compiler_params=pltpu.CompilerParams(vmem_limit_bytes=60 * 2**20),
    )(v, r)


N_COPIES = 14 + 8 + 8 + 3 + 4 + 8 + 10 + 5 + 17 + 8 + 5


def vmem(*shape):
    return pltpu.VMEM(shape, F32)


def v_cycle(rhs, cf, cm, cl):
    hbm = pl.BlockSpec(memory_space=pl.ANY)
    shape = jax.ShapeDtypeStruct((16, 4, 32, 128), F32)
    fine_t = (28, 4, 48, 128)
    fine_a = (28, 6, 4, 8, 128)
    mid_t = (24, 2, 32, 128)
    mid_a = (24, 4, 2, 8, 128)
    scratch = [
        vmem(*rhs.shape), vmem(*cf.shape), vmem(*cm.shape), vmem(*cl.shape),
        pltpu.SemaphoreType.DMA((5,)), pltpu.SemaphoreType.DMA((2, 16)),
        vmem(*fine_t), vmem(*fine_t), vmem(*fine_t), vmem(*fine_t),
        vmem(2, 3, 8, 4, 8, 128), vmem(2, 4, 16, 128), vmem(4, 4, 16, 128), vmem(4, 4, 8, 128),
        vmem(2, 3, 8, 4, 8, 128), vmem(2, 4, 16, 128), vmem(4, 4, 16, 128), vmem(4, 4, 8, 128),
        vmem(*fine_a), vmem(*fine_a), vmem(28, 7, 4, 8, 128), vmem(28, 6, 5, 8, 128),
        vmem(*fine_a), vmem(*fine_a), vmem(*fine_a), vmem(28, 6, 2, 8, 128), vmem(28, 6, 2, 8, 128),
        vmem(2, *mid_t), vmem(*mid_t), vmem(*mid_t), vmem(*mid_t),
        vmem(*mid_a), vmem(*mid_a), vmem(24, 5, 2, 8, 128), vmem(24, 4, 3, 8, 128),
        vmem(*mid_a), vmem(*mid_a), vmem(*mid_a), vmem(24, 4, 1, 8, 128), vmem(24, 4, 1, 8, 128),
        vmem(8, 2, 32, 128), vmem(4, 16, 128),
        vmem(2, 40, 4, 8, 128), vmem(4, 8, 128), vmem(40, 4, 8, 128), vmem(42, 4, 8, 128),
        vmem(20, 4, 2, 7, 8, 128), vmem(2, 20, 4, 8, 128), vmem(20, 4, 8, 128), vmem(20, 4, 8, 128), vmem(12, 48, 128),
        vmem(2, 1, 8, 4, 8, 128), vmem(2, 4, 16, 128), vmem(4, 4, 16, 128),
        vmem(2, 1, 8, 4, 8, 128), vmem(2, 4, 16, 128), vmem(4, 4, 16, 128),
        pltpu.SemaphoreType.DMA((N_COPIES,)), pltpu.SemaphoreType.DMA((N_COPIES,)),
    ]
    return pl.pallas_call(
        kernel,
        out_shape=(shape, shape),
        in_specs=[hbm] * 4,
        out_specs=(hbm, hbm),
        scratch_shapes=scratch,
        compiler_params=pltpu.CompilerParams(
            collective_id=0, has_side_effects=True, vmem_limit_bytes=60 * 2**20),
    )(rhs, cf, cm, cl)


def shift_kernel(k, cm, cl, out_m, out_l, send, recv):
    w, n = lax.axis_index("wide"), lax.axis_index("narrow")
    barrier = pltpu.get_barrier_semaphore()
    pl.semaphore_signal(barrier, inc=1, device_id=(lax.rem(w + k, NW), n), device_id_type=MESH)
    pl.semaphore_wait(barrier, 1)
    copies = [
        pltpu.make_async_remote_copy(
            src_ref=src, dst_ref=dst, send_sem=send.at[i], recv_sem=recv.at[i],
            device_id=(lax.rem(w + (NW - k), NW), n), device_id_type=MESH)
        for i, (src, dst) in enumerate(((cm, out_m), (cl, out_l)))]
    for copy in copies:
        copy.start()
    for copy in copies:
        copy.wait()


def on_device(rhs, cf, cm, cl, offset):
    def moved(k):
        return lambda a, b: pl.pallas_call(
            functools.partial(shift_kernel, k),
            out_shape=(jax.ShapeDtypeStruct(a.shape, F32), jax.ShapeDtypeStruct(b.shape, F32)),
            in_specs=[pl.BlockSpec(memory_space=pl.ANY)] * 2,
            out_specs=(pl.BlockSpec(memory_space=pl.ANY),) * 2,
            scratch_shapes=[pltpu.SemaphoreType.DMA((2,)), pltpu.SemaphoreType.DMA((2,))],
            compiler_params=pltpu.CompilerParams(collective_id=k, has_side_effects=True),
        )(a, b)

    cm, cl = lax.switch(offset[0] - 1, [moved(k) for k in range(1, NW)], cm, cl)
    return join(*v_cycle(rhs, cf, cm, cl))


def solution(mesh):
    return jax.shard_map(
        on_device,
        mesh=mesh,
        in_specs=(
            P("wide", "narrow", None),
            P(None, "wide", "narrow", None),
            P(None, "wide", "narrow", None),
            P(None, "wide", "narrow", None),
            P(),
        ),
        out_specs=(P("wide", "narrow", None), P("wide", "narrow", None)),
        check_vma=False,
    )
```

```python
import functools

import jax
import jax.numpy as jnp
from jax import lax
from jax.experimental import pallas as pl
from jax.experimental.pallas import tpu as pltpu
from jax.sharding import PartitionSpec as P

MESH = pl.DeviceIdType.MESH
F32 = jnp.float32
NW, NN = 32, 4
LOW_SENDS = [(dw, dn) for dw in (-4, 4, -2, 2, 0) for dn in (-1, 0, 1, 2)
             if (dw, dn) not in ((0, 0), (-4, 2), (4, 2))]
CORNERS = [(dw, dn) for dw in (-1, 1) for dn in (-1, 1)]
SIDES = [(-1, 0), (1, 0), (0, -1), (0, 1)]
GREETED = SIDES + CORNERS + [(-2, 0), (2, 0), (-4, 0), (4, 0), (0, 2)]
NEAR = [(dx, dy) for dx in range(1, 5) for dy in range(1, 5)]
CORNER_BC = [(f, dx, dy) for f in (0, 1) for dx, dy in NEAR if dx + dy <= 5 - f]
CORNER_S = [(0, dx, dy) for dx, dy in NEAR if dx + dy <= 4]
CORNER_V = [(0, dx, dy) for dx, dy in NEAR if dx + dy <= 5]


def iota(axis):
    return lax.broadcasted_iota(jnp.int32, (8, 128), axis)


def take(x, index):
    return jnp.take_along_axis(x, index, axis=1, mode="promise_in_bounds")


def swap(first, second, bit):
    low = iota(1) & bit == 0
    return (jnp.where(low, first, pltpu.roll(second, bit, 1)),
            jnp.where(low, pltpu.roll(first, 128 - bit, 1), second))


def split_lanes(parts):
    a, b = swap(parts[0], parts[1], 1)
    c, d = swap(parts[2], parts[3], 1)
    (a, c), (b, d) = swap(a, c, 2), swap(b, d, 2)
    return [a, b, c, d]


def join_lanes(tiles):
    a, b, c, d = tiles
    (a, c), (b, d) = swap(a, c, 2), swap(b, d, 2)
    a, b = swap(a, b, 1)
    c, d = swap(c, d, 1)
    return [a, b, c, d]


def place_index():
    lane = iota(1)
    return 32 * (lane % 4) + lane // 4


def down(x):
    return pltpu.roll(x, 1, 0)


def up(x):
    return pltpu.roll(x, 7, 0)


def left(x):
    return jnp.where(iota(1) < 4, pltpu.roll(x, 5, 1), pltpu.roll(x, 4, 1))


def right(x):
    return jnp.where(iota(1) >= 124, pltpu.roll(x, 123, 1), pltpu.roll(x, 124, 1))


class Level:
    def __init__(self, J, T, h, fx, fy, fz, rinv, diag, src, v):
        self.J, self.T = J, T
        self.h, self.fx, self.fy, self.fz = h, fx, fy, fz
        self.rinv, self.diag, self.src, self.v = rinv, diag, src, v

    def unroll(self, steps):
        return 1 if self.T == 4 else 2 if steps % 2 == 0 else 3 if steps % 3 == 0 else 1

    def cells(self, parity):
        return [(j, t) for j in range(self.J) for t in range(self.T) if (j + t) % 2 == parity]

    def setup(self, b_of, c_of, first, count, plane_lo, plane_hi, row_lo, row_hi):
        J, T = self.J, self.T
        lane = iota(1)
        row = J * iota(0)
        zero = jnp.zeros((8, 128), F32)

        def fill(x, _):
            scale = jnp.where((x >= plane_lo) & (x < plane_hi), 0.5, 0.0).astype(F32)
            for j in range(J):
                inside = (row + j >= row_lo) & (row + j < row_hi)
                for t in range(T):
                    self.h[x, j, t] = jnp.where(inside, b_of(x, j, t) * scale, zero)
            return 0

        lax.fori_loop(first - 1, first + count + 1, fill, 0)

        def open_face(x):
            return jnp.where((x == plane_lo) | (x == plane_hi), 0.0, 1.0).astype(F32)

        for j in range(J):
            for t in range(T):
                self.fx[first, j, t] = (self.h[first - 1, j, t] + self.h[first, j, t]) * open_face(first)

        def build(x, _):
            h = {(j, t): self.h[x, j, t] for j in range(J) for t in range(T)}
            edge_hi = open_face(x + 1)
            for t in range(T):
                real_y = [h[j, t] + (h[j - 1, t] if j else down(h[J - 1, t])) for j in range(J)]
                real_y.append(up(real_y[0]))
                for j in range(J + 1):
                    closed = (row + j == row_lo) | (row + j == row_hi)
                    self.fy[x, j, t] = jnp.where(closed, zero, real_y[j])
                for j in range(J):
                    here = h[j, t]
                    lo_x = self.h[x - 1, j, t] + here
                    hi_x = self.h[x + 1, j, t] + here
                    self.fx[x + 1, j, t] = hi_x * edge_hi
                    if t:
                        lo_z = here + h[j, t - 1]
                        self.fz[x, j, t] = lo_z
                    else:
                        beside = jnp.where(lane == 0, zero, left(h[j, T - 1]))
                        lo_z = here + beside
                        self.fz[x, j, t] = jnp.where(lane == 0, zero, lo_z)
                    if t < T - 1:
                        hi_z = here + h[j, t + 1]
                    else:
                        beside = jnp.where(lane == 127, zero, right(h[j, 0]))
                        hi_z = here + beside
                        self.fz[x, j, T] = jnp.where(lane == 127, zero, hi_z)
                    diag = lo_x + hi_x + real_y[j] + real_y[j + 1] + lo_z + hi_z + c_of(x, j, t)
                    self.diag[x, j, t] = diag
                    self.rinv[x, j, t] = 1.0 / diag
            return 0

        lax.fori_loop(first, first + count, build, 0, unroll=self.unroll(count))

    def pulled(self, x, j, t, planes):
        J, T = self.J, self.T
        get = planes[1]
        total = self.fx[x, j, t] * planes[0](j, t) + self.fx[x + 1, j, t] * planes[2](j, t)
        total += self.fy[x, j, t] * (get(j - 1, t) if j else down(get(J - 1, t)))
        total += self.fy[x, j + 1, t] * (get(j + 1, t) if j < J - 1 else up(get(0, t)))
        total += self.fz[x, j, t] * (get(j, t - 1) if t else left(get(j, T - 1)))
        total += self.fz[x, j, t + 1] * (get(j, t + 1) if t < T - 1 else right(get(j, 0)))
        return total

    def readers(self, x, parity):
        return [self.reader(x + k, (parity + k) % 2) for k in (-1, 0, 1, 2)]

    def reader(self, x, parity):
        seen = {}

        def get(j, t):
            if (j, t) not in seen:
                seen[j, t] = self.v[(parity + j + t) % 2][x, j, t // 2]
            return seen[j, t]

        return get

    def start(self, first, count):
        def body(i, _):
            for half in (0, 1):
                x = first + 2 * i + half
                for j, t in self.cells((first + half) % 2):
                    self.v[0][x, j, t // 2] = self.src[x, j, t] * self.rinv[x, j, t]
            return 0

        lax.fori_loop(0, count // 2, body, 0, unroll=self.unroll(count // 2))

    def half_sweep(self, colour, first, count):
        def body(i, _):
            planes = self.readers(first + 2 * i, first % 2)
            for half in (0, 1):
                x = first + 2 * i + half
                for j, t in self.cells((first + half + colour) % 2):
                    total = self.src[x, j, t] + self.pulled(x, j, t, planes[half:half + 3])
                    self.v[colour][x, j, t // 2] = total * self.rinv[x, j, t]
            return 0

        lax.fori_loop(0, count // 2, body, 0, unroll=self.unroll(count // 2))

    def residual(self, x, j, t, planes):
        return self.src[x, j, t] - (self.diag[x, j, t] * planes[1](j, t) - self.pulled(x, j, t, planes))

    def restrict_pair(self, x):
        sums = {}
        planes = self.readers(x, 0)
        for half in (0, 1):
            for j in range(self.J):
                for t in range(self.T):
                    value = self.residual(x + half, j, t, planes[half:half + 3])
                    key = (j // 2, t // 2)
                    sums[key] = sums[key] + value if key in sums else value
        return {key: 0.5 * value for key, value in sums.items()}


def kernel(rhs_hbm, cf_hbm, cm_hbm, cl_hbm, hbm_v, hbm_r,
           rhs, cf, cm, cl, in_sem, out_sem,
           tb, tc, ts, tv, pk, pk5, pkc, pkcs, py, py5, pc, pcs,
           fh, ffx, ffy, ffz, frinv, fdiag, fsrc, fv0, fv1,
           mt, st, vt, vp, mh, mfx, mfy, mfz, mrinv, mdiag, msrc, mv0, mv1, mstage, lstage,
           lc, s2own, s2g, lh, lcoef, lsrc, lv0, lv1, v2t,
           pkv, pkv5, pkvc, pyv, pyv5, pcv,
           send, recv):
    w = lax.axis_index("wide")
    n = lax.axis_index("narrow")
    core = lax.rem(w, 2)

    def device(dw, dn):
        return (lax.rem(w + (dw + NW), NW), lax.rem(n + (dn + NN), NN))

    loads = [pltpu.make_async_copy(cf_hbm.at[0], cf.at[0], in_sem.at[0]),
             pltpu.make_async_copy(cf_hbm.at[1], cf.at[1], in_sem.at[1]),
             pltpu.make_async_copy(rhs_hbm, rhs, in_sem.at[2]),
             pltpu.make_async_copy(cm_hbm, cm, in_sem.at[3]),
             pltpu.make_async_copy(cl_hbm, cl, in_sem.at[4])]
    for load in loads:
        load.start()
    ones, zeros = jnp.ones((8, 128), F32), jnp.zeros((8, 128), F32)
    for x in (*range(8), *range(32, 40)):
        for r in range(4):
            lc[0, x, r] = ones
            lc[1, x, r] = ones
            s2g[x, r] = zeros
    barrier = pltpu.get_barrier_semaphore()
    for dw, dn in GREETED:
        pl.semaphore_signal(barrier, inc=1, device_id=device(dw, dn), device_id_type=MESH)

    count = [0]

    def remote(src, dst, dw, dn):
        k = count[0]
        count[0] += 1
        copy = pltpu.make_async_remote_copy(
            src_ref=src, dst_ref=dst, send_sem=send.at[k], recv_sem=recv.at[k],
            device_id=device(dw, dn), device_id_type=MESH)
        copy.start()
        return copy

    def landed(copies):
        for copy in copies:
            copy.wait_recv()

    everything = []

    def to_split(read, target):
        def body(x, _):
            for r in range(4):
                parts = [read(x, r, a) for a in range(4)]
                for t, tile in enumerate(split_lanes(parts)):
                    target[6 + x, t, 8 + 8 * r:16 + 8 * r, :] = tile
            return 0

        lax.fori_loop(0, 16, body, 0)

    def pack(field, packed, which):
        def body(p, _):
            for t in range(4):
                for half in (0, 1):
                    x = 6 + 2 * p + half
                    packed[0, which, p, t, 4 * half:4 * half + 4, :] = field[x, t, 8:12, :]
                    packed[1, which, p, t, 4 * half:4 * half + 4, :] = field[x, t, 36:40, :]
            return 0

        lax.fori_loop(0, 8, body, 0)

    def pack_fifth(field, packed):
        def body(x, _):
            for t in range(4):
                packed[0, t, pl.ds(x, 1), :] = field[6 + x, t, 12:13, :]
                packed[1, t, pl.ds(x, 1), :] = field[6 + x, t, 35:36, :]
            return 0

        lax.fori_loop(0, 16, body, 0)

    def send_planes(field, layers):
        own = pl.ds(8, 32)
        return [
            remote(field.at[pl.ds(6, layers), :, own], field.at[pl.ds(22, layers), :, own], -1, 0),
            remote(field.at[pl.ds(22 - layers, layers), :, own], field.at[pl.ds(6 - layers, layers), :, own], 1, 0),
        ]

    def pack_corners(fields, rows, packed):
        def body(corner, _):
            cw, cn = corner // 2, corner % 2
            for r, (f, dx, dy) in enumerate(rows):
                x = 5 + dx + cw * (17 - 2 * dx)
                y = 7 + dy + cn * (33 - 2 * dy)
                for t in range(4):
                    packed[corner, t, r:r + 1, :] = fields[f][x, t, pl.ds(y, 1), :]
            return 0

        lax.fori_loop(0, 4, body, 0)

    def unpack_corners(fields, rows, got):
        def body(corner, _):
            cw, cn = corner // 2, corner % 2
            for r, (f, dx, dy) in enumerate(rows):
                x = 6 - dx + cw * (15 + 2 * dx)
                y = 8 - dy + cn * (31 + 2 * dy)
                for t in range(4):
                    fields[f][x, t, pl.ds(y, 1), :] = got[corner, t, r:r + 1, :]
            return 0

        lax.fori_loop(0, 4, body, 0)

    def send_corners(corner, got_corner):
        copies = []
        for dw, dn in CORNERS:
            here = (dw + 1) + (dn + 1) // 2
            copies.append(remote(corner.at[here], got_corner.at[3 - here], dw, dn))
        return copies

    def send_rows(packed, got):
        return [remote(packed.at[0], got.at[1], 0, -1), remote(packed.at[1], got.at[0], 0, 1)]

    def unpack(field, got, which):
        def place(x, t, half, lower, upper):
            field[x, t, 4:8, :] = lower[4 * half:4 * half + 4]
            field[x, t, 40:44, :] = upper[4 * half:4 * half + 4]

        def body(p, _):
            for t in range(4):
                lower, upper = got[0, which, p, t], got[1, which, p, t]
                for half in (0, 1):
                    place(6 + 2 * p + half, t, half, lower, upper)
            return 0

        lax.fori_loop(0, 8, body, 0)

    def unpack_fifth(field, got5):
        def body(x, _):
            for t in range(4):
                field[6 + x, t, 3:4, :] = got5[0, t, pl.ds(x, 1), :]
                field[6 + x, t, 44:45, :] = got5[1, t, pl.ds(x, 1), :]
            return 0

        lax.fori_loop(0, 16, body, 0)

    loads[0].wait()
    to_split(lambda x, r, a: cf[0, x, 8 * r:8 * r + 8, 128 * a:128 * a + 128], tb)
    pl.semaphore_wait(barrier, len(GREETED))
    pack(tb, pk, 2)
    round0_coef = send_rows(pk.at[:, 2], py.at[:, 2])
    round0_coef += send_planes(tb, 5)
    pack_fifth(tb, pk5)
    round0_coef += send_rows(pk5, py5)
    loads[1].wait()
    to_split(lambda x, r, a: cf[1, x, 8 * r:8 * r + 8, 128 * a:128 * a + 128], tc)
    pack(tc, pk, 1)
    round0_coef += send_rows(pk.at[:, 1], py.at[:, 1])
    round0_coef += send_planes(tc, 4)
    pack_corners((tb, tc), CORNER_BC, pkc)
    round0_coef += send_corners(pkc, pc)
    loads[4].wait()
    for which in (0, 1):
        for x in range(4):
            lc[which, 16 + 4 * core + x, n] = cl[which, x]
    coef_rows = []
    for dn in (1, 3, 2):
        mine = lc.at[:, pl.ds(16 + 4 * core, 4), n]
        coef_rows.append(remote(mine, mine, 0, dn))
    everything += coef_rows

    loads[2].wait()
    to_split(lambda x, r, a: rhs[x, 8 * r:8 * r + 8, 128 * a:128 * a + 128], ts)
    pack(ts, pk, 0)
    round0_src = send_rows(pk.at[:, 0], py.at[:, 0])
    round0_src += send_planes(ts, 4)
    pack_corners((ts,), CORNER_S, pkcs)
    round0_src += send_corners(pkcs, pcs)
    round0 = round0_coef + round0_src

    place = place_index()

    def split_mid(x, _):
        for which in (0, 1):
            for r in range(2):
                low, high = [cm[which, x, 8 * r:8 * r + 8, 128 * a:128 * a + 128] for a in range(2)]
                for t in range(2):
                    index = (2 * place + t) % 128
                    tile = jnp.where(place < 64, take(low, index), take(high, index))
                    mt[which, 8 + x, t, 8 + 8 * r:16 + 8 * r, :] = tile
        return 0

    loads[3].wait()
    lax.fori_loop(0, 8, split_mid, 0)

    def mid_slices(dw, dn, depth=8):
        depth = 8 if dw == 0 else depth
        planes = pl.ds(16 - depth if dw > 0 else 8, depth)
        planes_there = pl.ds(8 if dw == 0 else 16 if dw < 0 else 8 - depth, depth)
        rows = pl.ds(8, 16) if dn == 0 else pl.ds(8 if dn < 0 else 16, 8)
        rows_there = pl.ds(8, 16) if dn == 0 else pl.ds(24 if dn < 0 else 0, 8)
        return planes, rows, planes_there, rows_there

    def send_mid(field, depth):
        copies = []
        for dw, dn in SIDES + CORNERS:
            planes, rows, planes_there, rows_there = mid_slices(dw, dn, depth)
            copies.append(remote(field.at[planes, :, rows], field.at[planes_there, :, rows_there], dw, dn))
        return copies

    def send_low(src, dst_of):
        return [remote(src, dst_of(4 - dw + core), dw, dn) for dw, dn in LOW_SENDS]

    landed(round0_coef)
    mid_coef_copies = []
    for dw, dn in SIDES + CORNERS:
        planes, rows, planes_there, rows_there = mid_slices(dw, dn, 7)
        mid_coef_copies.append(remote(mt.at[:, planes, :, rows], mt.at[:, planes_there, :, rows_there], dw, dn))
    everything += mid_coef_copies

    landed(coef_rows)

    def send_low_coef(dw, rows):
        src = lc.at[:, pl.ds(16 + 4 * core, 4), rows]
        return remote(src, lc.at[:, pl.ds(4 * (4 - dw + core), 4), rows], dw, 0)

    low_coef_near = [send_low_coef(dw, pl.ds(0, 4)) for dw in (-2, 2)]
    low_coef_far = [send_low_coef(dw, pl.ds(n // 2, 3)) for dw in (-4, 4)]
    everything += low_coef_near + low_coef_far
    unpack(tb, py, 2)
    unpack(tc, py, 1)
    unpack_fifth(tb, py5)
    unpack_corners((tb, tc), CORNER_BC, pc)

    row_lo = lambda rows: jnp.where(n == 0, rows, 0)
    row_hi = lambda edge, last: jnp.where(n == NN - 1, edge, last)
    first_box, last_box = w == 0, w == NW - 1

    fine = Level(6, 4, fh, ffx, ffy, ffz, frinv, fdiag, fsrc, (fv0, fv1))
    fine.setup(
        lambda x, j, t: tb[x, t, pl.ds(j, 8, stride=6), :],
        lambda x, j, t: tc[x, t, pl.ds(j, 8, stride=6), :],
        2, 24,
        jnp.where(first_box, 6, -1), jnp.where(last_box, 22, 99),
        row_lo(8), row_hi(40, 48))

    landed(round0_src)

    unpack(ts, py, 0)
    unpack_corners((ts,), CORNER_S, pcs)

    def load_fine(q, _):
        for half in (0, 1):
            x = 2 + 2 * q + half
            for j in range(6):
                for t in range(4):
                    value = ts[x, t, pl.ds(j, 8, stride=6), :]
                    fsrc[x, j, t] = value
                    if (half + j + t) % 2 == 0:
                        fv0[x, j, t // 2] = value * frinv[x, j, t]
        return 0

    lax.fori_loop(0, 12, load_fine, 0)
    fine.half_sweep(1, 3, 22)

    fine.half_sweep(0, 4, 20)
    fine.half_sweep(1, 5, 18)

    def restrict_fine(i, _):
        for (j, t), value in fine.restrict_pair(6 + 2 * i).items():
            mstage[i, t, pl.ds(4 + j, 8, stride=3), :] = value
        for t in range(2):
            st[8 + i, t, 8:24, :] = mstage[i, t, 8:24, :]
        return 0

    lax.fori_loop(0, 8, restrict_fine, 0)

    round1 = send_mid(st, 6)
    everything += round1

    landed(mid_coef_copies)
    mid = Level(4, 2, mh, mfx, mfy, mfz, mrinv, mdiag, msrc, (mv0, mv1))
    mid.setup(
        lambda x, j, t: mt[0, x, t, pl.ds(j, 8, stride=4), :],
        lambda x, j, t: mt[1, x, t, pl.ds(j, 8, stride=4), :],
        1, 22,
        jnp.where(first_box, 8, -1), jnp.where(last_box, 16, 99),
        row_lo(8), row_hi(24, 32))

    landed(round1)

    def load_mid(x, _):
        for j in range(4):
            for t in range(2):
                msrc[x, j, t] = st[x, t, pl.ds(j, 8, stride=4), :]
        return 0

    lax.fori_loop(2, 22, load_mid, 0)
    mid.start(4, 16)
    mid.half_sweep(1, 5, 14)
    mid.half_sweep(0, 6, 12)
    mid.half_sweep(1, 7, 10)

    natural = 4 * (iota(1) % 32) + iota(1) // 32

    def restrict_mid(i, _):
        for (j, t), value in mid.restrict_pair(8 + 2 * i).items():
            lstage[i, pl.ds(j, 8, stride=2), :] = value
        value = take(lstage[i, 4:12, :], natural)
        s2own[i] = value
        s2g[16 + 4 * core + i, n] = value
        return 0

    lax.fori_loop(0, 4, restrict_mid, 0)

    def to_sibling(refs_of, boxes):
        copies = []
        for box in boxes:
            part = refs_of(pl.ds(8 * box + 4 * core, 4))
            k = count[0]
            count[0] += 1
            copy = pltpu.make_async_remote_copy(
                src_ref=part, dst_ref=part, send_sem=send.at[k], recv_sem=recv.at[k],
                device_id=(w + 1 - 2 * core, n), device_id_type=MESH)
            copy.start()
            copies.append(copy)
        return copies

    round2 = send_low(s2own, lambda slot: s2g.at[pl.ds(4 * slot, 4), n])
    everything += round2

    def store_mid(q, _):
        for half in (0, 1):
            x = 2 * q + half
            get = mid.reader(8 + x, half)
            for j in range(4):
                for t in range(2):
                    mstage[x, t, pl.ds(j, 8, stride=4), :] = get(j, t)
            for t in range(2):
                vt[8 + x, t, 8:24, :] = mstage[x, t, 8:24, :]
        return 0

    lax.fori_loop(0, 4, store_mid, 0)
    landed(low_coef_near + low_coef_far)
    low_coef_shared = to_sibling(lambda planes: lc.at[:, planes], range(5))
    everything += low_coef_shared

    mid_copies = send_mid(vt, 8)
    everything += mid_copies

    def store_fine(q, _):
        for half in (0, 1):
            x = 6 + 2 * q + half
            get = fine.reader(x, half)
            for j in range(6):
                for t in range(4):
                    tv[x, t, pl.ds(j, 8, stride=6), :] = get(j, t)
        return 0

    lax.fori_loop(0, 8, store_fine, 0)
    pack(tv, pkv, 0)
    pack_fifth(tv, pkv5)
    pack_corners((tv,), CORNER_V, pkvc)
    fine_copies = send_planes(tv, 5) + send_rows(pkv.at[:, 0], pyv.at[:, 0]) + send_rows(pkv5, pyv5)
    fine_copies += send_corners(pkvc, pcv)
    everything += fine_copies

    landed(low_coef_shared)
    lane, sub = iota(1), iota(0)
    par = (lane + sub) % 2 == 0
    zero = jnp.zeros((8, 128), F32)
    low_lo = 16 - 4 * (w - core)
    low_hi = low_lo + 4 * NW

    for r in range(4):
        lh[0, r] = zero
        lh[41, r] = zero

    def fill_low(i, _):
        scale = jnp.where((i >= low_lo) & (i < low_hi), 0.5, 0.0).astype(F32)
        for r in range(4):
            lh[1 + i, r] = lc[0, i, r] * scale
        return 0

    lax.fori_loop(0, 40, fill_low, 0, unroll=4)

    def open_low(i):
        return jnp.where((i == low_lo) | (i == low_hi), 0.0, 1.0).astype(F32)

    def build_low(q, _):
        p = q + 2 * core
        i = 2 * p
        edge_lo, edge_hi = open_low(i), open_low(i + 2)
        h = [[lh[i + k, r] for r in range(4)] for k in range(4)]
        for r in range(4):
            lo_x = h[0][r] + h[1][r]
            in_x = h[1][r] + h[2][r]
            hi_x = h[2][r] + h[3][r]
            faces, diags = [], []
            for k in (1, 2):
                here = h[k][r]
                below = jnp.where(sub == 0, down(h[k][r - 1]) if r else zero, down(here))
                above = jnp.where(sub == 7, up(h[k][r + 1]) if r < 3 else zero, up(here))
                lo_y, hi_y = here + below, here + above
                lo_z = here + jnp.where(lane == 0, zero, pltpu.roll(here, 1, 1))
                hi_z = here + jnp.where(lane == 127, zero, pltpu.roll(here, 127, 1))
                out_x = lo_x if k == 1 else hi_x
                diags.append(in_x + out_x + lo_y + hi_y + lo_z + hi_z + lc[1, i + k - 1, r])
                if r == 0:
                    lo_y = jnp.where(sub == 0, zero, lo_y)
                if r == 3:
                    hi_y = jnp.where(sub == 7, zero, hi_y)
                faces.append((out_x * (edge_lo if k == 1 else edge_hi), lo_y, hi_y,
                              jnp.where(lane == 0, zero, lo_z), jnp.where(lane == 127, zero, hi_z)))
            for colour in (0, 1):
                lcoef[p, r, colour, 0] = in_x
                for k in range(5):
                    a, b = faces[colour][k], faces[1 - colour][k]
                    lcoef[p, r, colour, 1 + k] = jnp.where(par, a, b)
                lcoef[p, r, colour, 6] = 1.0 / jnp.where(par, diags[colour], diags[1 - colour])
        return 0

    lax.fori_loop(0, 18, build_low, 0)

    landed([copy for copy, (dw, dn) in zip(round2, LOW_SENDS) if abs(dw) < 4])
    source_shared = to_sibling(lambda planes: s2g.at[planes], (1, 2, 3))
    landed([copy for copy, (dw, dn) in zip(round2, LOW_SENDS) if abs(dw) == 4])
    source_shared += to_sibling(lambda planes: s2g.at[planes], (0, 4))
    everything += source_shared
    landed(source_shared)

    def load_low(q, _):
        p = q + 2 * core
        for r in range(4):
            a, b = s2g[2 * p, r], s2g[2 * p + 1, r]
            lsrc[0, p, r] = jnp.where(par, a, b)
            lsrc[1, p, r] = jnp.where(par, b, a)
            lv0[p, r] = lsrc[0, p, r] * lcoef[p, r, 0, 6]
        return 0

    lax.fori_loop(0, 18, load_low, 0, unroll=2)

    def low_half_sweep(colour, first, last):
        here, there = (lv0, lv1) if colour == 0 else (lv1, lv0)

        def body(q, _):
            first_pair = first + 2 * q + 2 * core
            seen = [[there[first_pair + k, r] for r in range(4)] for k in (-1, 0, 1, 2)]
            for k in (0, 1):
                p = first_pair + k
                before, other, after = seen[k:k + 3]
                downs = [down(value) for value in other]
                ups = [up(value) for value in other]
                for r in range(4):
                    coef = lambda which: lcoef[p, r, colour, which]
                    a, b = (before, after) if colour == 0 else (after, before)
                    total = lsrc[colour, p, r] + coef(0) * other[r] + coef(1) * jnp.where(par, a[r], b[r])
                    total += coef(2) * jnp.where(sub == 0, downs[r - 1], downs[r])
                    total += coef(3) * jnp.where(sub == 7, ups[(r + 1) % 4], ups[r])
                    total += coef(4) * pltpu.roll(other[r], 1, 1) + coef(5) * pltpu.roll(other[r], 127, 1)
                    here[p, r] = total * coef(6)
            return 0

        steps = (last + 1 - first) // 2
        lax.fori_loop(0, steps, body, 0, unroll=2 if steps % 2 == 0 else 3 if steps % 3 == 0 else 1)

    for k in range(2, 13):
        low_half_sweep((k + 1) % 2, k // 2, 17 - k // 2)

    for i in range(12):
        v2t[i, 0:8, :] = zero
        v2t[i, 40:48, :] = zero
    for p in range(6):
        for r in range(4):
            a, b = lv0[6 + 2 * core + p, r], lv1[6 + 2 * core + p, r]
            v2t[2 * p, 8 + 8 * r:16 + 8 * r, :] = jnp.where(par, a, b)
            v2t[2 * p + 1, 8 + 8 * r:16 + 8 * r, :] = jnp.where(par, b, a)

    landed(mid_copies)

    def correct_mid(i, _):
        for j in (0, 2):
            coarse = take(v2t[i, pl.ds(8 * n + 4 + j // 2, 8, stride=2), :], place)
            for half in (0, 1):
                for jj in (j, j + 1):
                    for t in range(2):
                        x = 2 * i + half
                        if (half + jj + t) % 2 == 1:
                            mv1[x, jj, t // 2] = vt[x, t, pl.ds(jj, 8, stride=4), :] + coarse
        return 0

    lax.fori_loop(0, 12, correct_mid, 0)
    mid.half_sweep(0, 2, 20)
    mid.half_sweep(1, 3, 18)
    mid.half_sweep(0, 4, 16)
    mid.half_sweep(1, 5, 14)

    def spread_mid(q, _):
        for half in (0, 1):
            x = 5 + 2 * q + half
            get = mid.reader(x, 1 - half)
            for j in range(4):
                for t in range(2):
                    vp[x, t, pl.ds(j, 8, stride=4), :] = get(j, t)
        return 0

    lax.fori_loop(0, 7, spread_mid, 0)

    landed(fine_copies)
    unpack(tv, pyv, 0)
    unpack_fifth(tv, pyv5)
    unpack_corners((tv,), CORNER_V, pcv)

    def correct_fine(q, _):
        for j in range(3):
            for t in range(2):
                coarse = vp[q + 5, t, pl.ds(4 + j, 8, stride=3), :]
                for half in (0, 1):
                    x = 2 * q + half
                    for jj in (2 * j, 2 * j + 1):
                        for tt in (2 * t, 2 * t + 1):
                            if (half + jj + tt) % 2 == 1:
                                fv1[x, jj, tt // 2] = tv[x, tt, pl.ds(jj, 8, stride=6), :] + coarse
        return 0

    lax.fori_loop(0, 14, correct_fine, 0)
    fine.half_sweep(0, 2, 24)
    fine.half_sweep(1, 3, 22)
    fine.half_sweep(0, 4, 20)
    fine.half_sweep(1, 5, 18)

    for copy in round0:
        copy.wait_send()

    def result(k, x):
        staged, hbm = ((ts, hbm_v), (tc, hbm_r))[k]
        return pltpu.make_async_copy(staged.at[6 + x, :, pl.ds(8, 32)], hbm.at[x], out_sem.at[k, x])

    def finish(q, _):
        planes = fine.readers(6 + 2 * q, 0)
        for half in (0, 1):
            x = 2 * q + half
            for j in range(6):
                for t in range(4):
                    ts[6 + x, t, pl.ds(j, 8, stride=6), :] = planes[1 + half](j, t)
                    tc[6 + x, t, pl.ds(j, 8, stride=6), :] = fine.residual(6 + x, j, t, planes[half:half + 3])
            result(0, x).start()
            result(1, x).start()
        return 0

    def settle(x, _):
        result(0, x).wait()
        result(1, x).wait()
        return 0

    lax.fori_loop(0, 8, finish, 0)
    lax.fori_loop(0, 16, settle, 0)
    for copy in everything:
        copy.wait_send()


def join_kernel(v_ref, r_ref, out_v, out_r):
    def body(x, _):
        for tiles_ref, out in ((v_ref, out_v), (r_ref, out_r)):
            for r in range(4):
                tiles = [tiles_ref[x, t, 8 * r:8 * r + 8, :] for t in range(4)]
                for a, part in enumerate(join_lanes(tiles)):
                    out[x, 8 * r:8 * r + 8, 128 * a:128 * a + 128] = part
        return 0

    lax.fori_loop(0, v_ref.shape[0], body, 0)


def join(v, r):
    shape = jax.ShapeDtypeStruct((16, 32, 512), F32)
    tiles = pl.BlockSpec((8, 4, 32, 128), lambda i: (i, 0, 0, 0))
    whole = pl.BlockSpec((8, 32, 512), lambda i: (i, 0, 0))
    return pl.pallas_call(
        join_kernel, grid=(2,), out_shape=(shape, shape),
        in_specs=[tiles] * 2, out_specs=(whole, whole),
        compiler_params=pltpu.CompilerParams(vmem_limit_bytes=60 * 2**20),
    )(v, r)


N_COPIES = 14 + 8 + 8 + 3 + 4 + 8 + 10 + 5 + 17 + 8 + 5


def vmem(*shape):
    return pltpu.VMEM(shape, F32)


def v_cycle(rhs, cf, cm, cl):
    hbm = pl.BlockSpec(memory_space=pl.ANY)
    shape = jax.ShapeDtypeStruct((16, 4, 32, 128), F32)
    fine_t = (28, 4, 48, 128)
    fine_a = (28, 6, 4, 8, 128)
    mid_t = (24, 2, 32, 128)
    mid_a = (24, 4, 2, 8, 128)
    scratch = [
        vmem(*rhs.shape), vmem(*cf.shape), vmem(*cm.shape), vmem(*cl.shape),
        pltpu.SemaphoreType.DMA((5,)), pltpu.SemaphoreType.DMA((2, 16)),
        vmem(*fine_t), vmem(*fine_t), vmem(*fine_t), vmem(*fine_t),
        vmem(2, 3, 8, 4, 8, 128), vmem(2, 4, 16, 128), vmem(4, 4, 16, 128), vmem(4, 4, 8, 128),
        vmem(2, 3, 8, 4, 8, 128), vmem(2, 4, 16, 128), vmem(4, 4, 16, 128), vmem(4, 4, 8, 128),
        vmem(*fine_a), vmem(*fine_a), vmem(28, 7, 4, 8, 128), vmem(28, 6, 5, 8, 128),
        vmem(*fine_a), vmem(*fine_a), vmem(*fine_a), vmem(28, 6, 2, 8, 128), vmem(28, 6, 2, 8, 128),
        vmem(2, *mid_t), vmem(*mid_t), vmem(*mid_t), vmem(*mid_t),
        vmem(*mid_a), vmem(*mid_a), vmem(24, 5, 2, 8, 128), vmem(24, 4, 3, 8, 128),
        vmem(*mid_a), vmem(*mid_a), vmem(*mid_a), vmem(24, 4, 1, 8, 128), vmem(24, 4, 1, 8, 128),
        vmem(8, 2, 32, 128), vmem(4, 16, 128),
        vmem(2, 40, 4, 8, 128), vmem(4, 8, 128), vmem(40, 4, 8, 128), vmem(42, 4, 8, 128),
        vmem(20, 4, 2, 7, 8, 128), vmem(2, 20, 4, 8, 128), vmem(20, 4, 8, 128), vmem(20, 4, 8, 128), vmem(12, 48, 128),
        vmem(2, 1, 8, 4, 8, 128), vmem(2, 4, 16, 128), vmem(4, 4, 16, 128),
        vmem(2, 1, 8, 4, 8, 128), vmem(2, 4, 16, 128), vmem(4, 4, 16, 128),
        pltpu.SemaphoreType.DMA((N_COPIES,)), pltpu.SemaphoreType.DMA((N_COPIES,)),
    ]
    return pl.pallas_call(
        kernel,
        out_shape=(shape, shape),
        in_specs=[hbm] * 4,
        out_specs=(hbm, hbm),
        scratch_shapes=scratch,
        compiler_params=pltpu.CompilerParams(
            collective_id=0, has_side_effects=True, vmem_limit_bytes=60 * 2**20),
    )(rhs, cf, cm, cl)


def shift_kernel(k, cm, cl, out_m, out_l, send, recv):
    w, n = lax.axis_index("wide"), lax.axis_index("narrow")
    barrier = pltpu.get_barrier_semaphore()
    pl.semaphore_signal(barrier, inc=1, device_id=(lax.rem(w + k, NW), n), device_id_type=MESH)
    pl.semaphore_wait(barrier, 1)
    copies = [
        pltpu.make_async_remote_copy(
            src_ref=src, dst_ref=dst, send_sem=send.at[i], recv_sem=recv.at[i],
            device_id=(lax.rem(w + (NW - k), NW), n), device_id_type=MESH)
        for i, (src, dst) in enumerate(((cm, out_m), (cl, out_l)))]
    for copy in copies:
        copy.start()
    for copy in copies:
        copy.wait()


def on_device(rhs, cf, cm, cl, offset):
    def moved(k):
        return lambda a, b: pl.pallas_call(
            functools.partial(shift_kernel, k),
            out_shape=(jax.ShapeDtypeStruct(a.shape, F32), jax.ShapeDtypeStruct(b.shape, F32)),
            in_specs=[pl.BlockSpec(memory_space=pl.ANY)] * 2,
            out_specs=(pl.BlockSpec(memory_space=pl.ANY),) * 2,
            scratch_shapes=[pltpu.SemaphoreType.DMA((2,)), pltpu.SemaphoreType.DMA((2,))],
            compiler_params=pltpu.CompilerParams(collective_id=k, has_side_effects=True),
        )(a, b)

    cm, cl = lax.switch(offset[0] - 1, [moved(k) for k in range(1, NW)], cm, cl)
    return join(*v_cycle(rhs, cf, cm, cl))


def solution(mesh):
    return jax.shard_map(
        on_device,
        mesh=mesh,
        in_specs=(
            P("wide", "narrow", None),
            P(None, "wide", "narrow", None),
            P(None, "wide", "narrow", None),
            P(None, "wide", "narrow", None),
            P(),
        ),
        out_specs=(P("wide", "narrow", None), P("wide", "narrow", None)),
        check_vma=False,
    )
```
